256 devices in a mesh: ctx: 32 (over z, y), head: 8 (over x, core).
Axes of the slice: x: 4, y: 4, z: 8, core: 2. Of those that a mesh axis runs over, the one named last changes fastest.
Arguments:
- prompt_hidden: bfloat16 [16384, 7168], P('ctx', 'head'), may hold values from -6 to 6
- latent_down: bfloat16 [7168, 512], P('head'), may hold values from -0.0625 to 0.0625
- rope_down: bfloat16 [64, 7168], P(None, 'head'), may hold values from -0.0625 to 0.0625
- latent_gain: float32 [512], replicated, may hold values from 0.1 to 1.9
- request_lengths: int32 [4], replicated, may hold values from 1 to 8192, 16384 in all
- row_request: int32 [128], replicated, may hold values from 0 to 3
- query_nope: bfloat16 [4, 128, 128, 128], P(None, 'ctx', 'head'), may hold values from -6 to 6
- query_rope: bfloat16 [4, 128, 128, 64], P(None, 'ctx', 'head'), may hold values from -100 to 100
- new_latent: bfloat16 [4, 128, 512], P(None, 'ctx'), may hold values from -6 to 6
- new_rope: bfloat16 [4, 128, 64], P(None, 'ctx'), may hold values from -4 to 4
- key_up: bfloat16 [128, 128, 512], P('head'), may hold values from -0.5 to 0.5
- value_up: bfloat16 [128, 512, 128], P('head'), may hold values from -0.25 to 0.25
Outputs:
- latent_cache: bfloat16 [16384, 512], P('ctx')
- rope_cache: bfloat16 [64, 16384], P(None, 'ctx')
- head_values: bfloat16 [4, 128, 128, 128], P(None, 'ctx', 'head')
The draws below stay inside these ranges and needn't reach their ends.
Inputs may be any that keep to these rules, and one draw needn't show every extreme that they name: `request_lengths`: the lengths sum to 16384; the longest is exactly 8192.
All inputs are finite; a program needn't handle non-finite values.
Results may differ from the reference program's by a relative error of at most 0.02.
Values may be sent and summed in bfloat16 or wider, within the bound.
A program may use at most 128 MiB of HBM per device.

```python
import math
import jax
import jax.numpy as jnp
import numpy as np
from jax import lax

D = 7168
HEADS = 128
LAT = 512
ROPE = 64
NOPE = 128
VDIM = 128
TOK_DEV = 512
ROWS = 128
STEPS = 4
REQS = 4
CTXLEN = 16384
N_CTX = 32


def draw_query_rope(key, part):
    key = jax.random.fold_in(key, 5)
    drawn = jnp.clip(jax.random.normal(key, (STEPS, ROWS, HEADS, ROPE), jnp.float32), -6.0, 6.0)
    return drawn.astype(jnp.bfloat16)


def draw_new_rope(key, part):
    key = jax.random.fold_in(key, 9)
    drawn = jnp.clip(jax.random.normal(key, (STEPS, ROWS, ROPE), jnp.float32), -4.0, 4.0)
    return drawn.astype(jnp.bfloat16)


def plant(drawn, stream_key, least, top_value):
    longest = drawn.shape.index(max(drawn.shape))
    spots = []
    for shift in (0, 1):
        where = [jax.random.randint(jax.random.fold_in(stream_key, axis), (), 0, length) for axis, length in enumerate(drawn.shape)]
        where[longest] = (where[longest] + shift) % drawn.shape[longest]
        spots.append(tuple(where))
    return drawn.at[spots[0]].set(least).at[spots[1]].set(top_value)


def level_of(stream_key, extent, pieces, least, high):
    level, own = 1.0, jax.random.fold_in(stream_key, 6)
    for dim, parts in pieces:
        draws = jnp.exp(jax.random.uniform(jax.random.fold_in(own, dim), (parts,), jnp.float32, least / len(pieces), high / len(pieces)))
        level = level * jnp.repeat(draws, extent[dim] // parts).reshape([-1 if axis == dim else 1 for axis in range(len(extent))])
    return level


def cumulative_ranks(count, slope):
    portions = [(1 << 20) // math.isqrt(standing ** slope) + 1 for standing in range(1, count + 1)]
    width = 1 + sum(portions) // (1 << 30)
    return np.cumsum(np.array([max(1, weight // width) for weight in portions]))


def ranked(own_key, shape, amount, lean):
    grid = cumulative_ranks(amount, lean)
    pick = jax.random.randint(jax.random.fold_in(own_key, 1), shape, 0, int(grid[amount - 1]))
    rank = jnp.searchsorted(jnp.asarray(grid, jnp.int32), pick, side="right")
    return jax.random.permutation(jax.random.fold_in(own_key, 2), amount)[rank].astype(jnp.int32)


def split_up(amount, total, bound, slope):
    weights = [(1 << 20) // math.isqrt(grade ** slope) + 1 for grade in range(2, amount + 1)]
    rest, given = total - bound - (amount - 1), [1] * (amount - 1)
    while rest > 0:
        free = [i for i in range(amount - 1) if given[i] < bound]
        mass, left = sum([weights[i] for i in free]), rest
        for i in free:
            extra = min(bound - given[i], max(1, left * weights[i] // mass), rest)
            given[i] = given[i] + extra
            rest = rest - extra
    return np.array([bound] + given)


def uneven(key, number_of, total, reach, skew):
    if number_of == 2:
        one = jax.random.randint(key, (), max(1, total - reach), min(reach, total - 1) + 1)
        return jnp.stack([one, total - one])
    tallies = jnp.asarray(split_up(number_of, total, reach, skew), jnp.int32)
    twos = (number_of - 1) // 2
    giver, receiver = tallies[1:1 + 2 * twos:2], tallies[2:2 + 2 * twos:2]
    room = jnp.minimum(giver - 1, reach - receiver)
    shifted = jax.random.randint(jax.random.fold_in(key, 1), (twos,), 0, 1 << 20) % (room + 1)
    tallies = tallies.at[1:1 + 2 * twos:2].set(giver - shifted).at[2:2 + 2 * twos:2].set(receiver + shifted)
    return tallies[jax.random.permutation(jax.random.fold_in(key, 2), number_of)]


def gaussian(own_key, extent, width, reach, shards=(), held_as=jnp.bfloat16):
    entries = jax.random.normal(own_key, extent, jnp.float32) * width
    if len(shards) > 0:
        entries = level_of(own_key, extent, shards, -0.22, 0.18) * entries
    return jnp.clip(entries, min=-reach, max=reach).astype(held_as)


def setup_inputs(seed: int = 0) -> dict:
    key_of = jax.random.split(jax.random.key(seed), 13)
    prompt_hidden = gaussian(key_of[0], (CTXLEN, D), 1.0, 6.0, ((0, 32), (1, 8)))
    latent_down = gaussian(key_of[1], (D, LAT), D ** -0.5, 0.0625, ((0, 8),))
    rope_down = gaussian(key_of[2], (ROPE, D), D ** -0.5, 0.0625, ((1, 8),))
    latent_gain = jnp.clip(1.0 + 0.18 * jax.random.normal(key_of[3], (LAT,), jnp.float32), 0.1, 1.9)
    request_lengths = uneven(key_of[4], REQS, CTXLEN, CTXLEN // 2, 2).astype(jnp.int32)
    row_request = plant(ranked(key_of[5], (ROWS,), REQS, 2), jax.random.fold_in(key_of[5], 3), 0, REQS - 1).astype(jnp.int32)
    query_nope = gaussian(key_of[6], (STEPS, ROWS, HEADS, NOPE), 1.0, 6.0, ((1, 32), (2, 8)))
    query_rope = draw_query_rope(jax.random.fold_in(key_of[12], 71), 0)
    new_latent = gaussian(key_of[8], (STEPS, ROWS, LAT), 1.0, 6.0, ((1, 32),))
    new_rope = draw_new_rope(jax.random.fold_in(key_of[12], 71), 0)
    key_up = gaussian(key_of[10], (HEADS, NOPE, LAT), NOPE ** -0.5, 0.5, ((0, 8),))
    value_up = gaussian(key_of[11], (HEADS, LAT, VDIM), LAT ** -0.5, 0.25, ((0, 8),))
    return dict(prompt_hidden=prompt_hidden, latent_down=latent_down, rope_down=rope_down, latent_gain=latent_gain, request_lengths=request_lengths, row_request=row_request, query_nope=query_nope, query_rope=query_rope, new_latent=new_latent, new_rope=new_rope, key_up=key_up, value_up=value_up)


epsilon = 1e-06
masked_score = -1e+30

def owners(positions, request_lengths):
    end_points = jnp.cumsum(request_lengths, dtype=jnp.int32)
    starts = end_points - request_lengths
    inside = (positions[:, None] >= starts[None, :]) & (positions[:, None] < end_points[None, :])
    numbers = jnp.arange(request_lengths.shape[0], dtype=jnp.int32)
    request_of = lax.optimization_barrier(jnp.sum(jnp.where(inside, numbers[None, :], 0), axis=1, dtype=jnp.int32))
    offset = positions - lax.optimization_barrier(jnp.sum(jnp.where(inside, starts[None, :], 0), axis=1, dtype=jnp.int32))
    return (request_of, offset)

def normalize(latent_sum, latent_gain):
    mean_square = lax.optimization_barrier(jnp.mean(latent_sum * latent_sum, axis=-1, keepdims=True))
    return (latent_sum * lax.rsqrt(mean_square + epsilon) * latent_gain).astype(jnp.bfloat16)

def rotate(rope_rows, offset):
    half_rows = rope_rows.shape[0] // 2
    frequency = 10000.0 ** (-2.0 * jnp.arange(half_rows, dtype=jnp.float32) / rope_rows.shape[0])
    angles = frequency[:, None] * offset.astype(jnp.float32)[None, :]
    cosine = jnp.cos(angles)
    sine_part = jnp.sin(angles)
    leading = rope_rows[:half_rows]
    trailing = rope_rows[half_rows:]
    rotated = jnp.concatenate([leading * cosine - trailing * sine_part, leading * sine_part + trailing * cosine], axis=0)
    return rotated.astype(jnp.bfloat16)

def block_weights(scores, allowed):
    block_max = lax.optimization_barrier(jnp.max(jnp.where(allowed, scores, masked_score), axis=-1))
    weights = jnp.where(allowed, jnp.exp(scores - block_max[..., None]), 0.0)
    return (weights, lax.optimization_barrier(jnp.sum(weights, axis=-1)), block_max)

def combine(carry, part):
    accum, total, running = carry
    lifted, part_total, part_max = part
    new_max = jnp.maximum(running, part_max)
    old_scale = jnp.exp(running - new_max)
    new_scale = jnp.exp(part_max - new_max)
    return (accum * old_scale[..., None] + lifted * new_scale[..., None], total * old_scale + part_total * new_scale, new_max)

def reference(prompt_hidden, latent_down, rope_down, latent_gain, request_lengths, row_request, query_nope, query_rope, new_latent, new_rope, key_up, value_up):
    latent_sum = jnp.dot(prompt_hidden, latent_down, preferred_element_type=jnp.float32)
    rope_sum = lax.dot_general(rope_down, prompt_hidden, (((1,), (1,)), ((), ())), preferred_element_type=jnp.float32)
    positions = jnp.arange(CTXLEN, dtype=jnp.int32)
    key_owner, offset = owners(positions, request_lengths)
    latent_cache = normalize(latent_sum, latent_gain)
    rope_cache = rotate(rope_sum, offset)
    scale = 1.0 / math.sqrt(NOPE + ROPE)
    absorbed = jnp.einsum('trhn,hnc->trhc', query_nope.astype(jnp.float32), key_up.astype(jnp.float32)).astype(jnp.bfloat16)
    absorbed_wide = absorbed.astype(jnp.float32)
    rope_wide = query_rope.astype(jnp.float32)
    flat_abs = absorbed_wide.reshape(STEPS * ROWS, HEADS, LAT)
    flat_rope = rope_wide.reshape(STEPS * ROWS, HEADS, ROPE)
    row_owner = jnp.tile(row_request, STEPS)
    value_wide = value_up.astype(jnp.float32)
    blocks_latent = latent_cache.reshape(N_CTX, TOK_DEV, LAT)
    blocks_rope = rope_cache.reshape(ROPE, N_CTX, TOK_DEV).transpose(1, 0, 2)
    blocks_owner = key_owner.reshape(N_CTX, TOK_DEV)

    def visit(carry, block):
        latent_block, rope_block, owner_block = block
        latent_block = latent_block.astype(jnp.float32)
        scores = (jnp.einsum('qhc,kc->qhk', flat_abs, latent_block) + jnp.einsum('qhp,pk->qhk', flat_rope, rope_block.astype(jnp.float32))) * scale
        allowed = (row_owner[:, None] == owner_block[None, :])[:, None, :]
        weights, total, block_max = block_weights(scores, allowed)
        mixed = jnp.einsum('qhk,kc->qhc', weights.astype(jnp.bfloat16).astype(jnp.float32), latent_block)
        lifted = jnp.einsum('qhc,hcv->qhv', mixed.astype(jnp.bfloat16).astype(jnp.float32), value_wide)
        return (combine(carry, (lifted, total, block_max)), None)
    start_carry = (jnp.zeros((STEPS * ROWS, HEADS, VDIM), jnp.float32), jnp.zeros((STEPS * ROWS, HEADS), jnp.float32), jnp.full((STEPS * ROWS, HEADS), masked_score, jnp.float32))
    carry, unused = lax.scan(visit, start_carry, (blocks_latent, blocks_rope, blocks_owner))
    fresh_latent = new_latent.astype(jnp.float32)
    fresh = (jnp.einsum('trhc,krc->trhk', absorbed_wide, fresh_latent) + jnp.einsum('trhp,krp->trhk', rope_wide, new_rope.astype(jnp.float32))) * scale
    step_index = jnp.arange(STEPS, dtype=jnp.int32)
    causal = (step_index[None, :] <= step_index[:, None])[:, None, None, :]
    fresh_weights, fresh_total, fresh_max = block_weights(fresh, causal)
    fresh_mixed = jnp.einsum('trhk,krc->trhc', fresh_weights.astype(jnp.bfloat16).astype(jnp.float32), fresh_latent)
    fresh_lifted = jnp.einsum('trhc,hcv->trhv', fresh_mixed.astype(jnp.bfloat16).astype(jnp.float32), value_wide)
    accum, total, running = combine(carry, (fresh_lifted.reshape(STEPS * ROWS, HEADS, VDIM), fresh_total.reshape(STEPS * ROWS, HEADS), fresh_max.reshape(STEPS * ROWS, HEADS)))
    head_values = (accum / total[..., None]).astype(jnp.bfloat16).reshape(STEPS, ROWS, HEADS, VDIM)
    return (latent_cache, rope_cache, head_values)
```

```python
import functools
import math

import jax
import jax.numpy as jnp
import numpy as np
from jax import lax
from jax.experimental import pallas as pl
from jax.experimental.pallas import tpu as pltpu
from jax.sharding import PartitionSpec as P

MESH = pl.DeviceIdType.MESH
EPSILON = 1e-6
MASKED = -1e30
Y_SIZE = 4
CORES = 2
LANES = 128
F32 = jnp.float32
BF16 = jnp.bfloat16


def nt(a, b):
    return lax.dot_general(a, b, (((1,), (1,)), ((), ())), preferred_element_type=F32)


def nn(a, b):
    return jnp.dot(a, b, preferred_element_type=F32)


def kernel(
    cfg,
    hid_h, ld_h, rd_h, gain_h, lens, rowreq, qn_h, qr_h, nl_h, nr_h, ku_h, vu_h, freq_h,
    lat_o, rope_o, hv_o,
    hid, ld, rd, gain, qn, qr, nl, nr, ku, vu, freq, loc,
    a_snd, a_rcv, part, b_snd, b_rcv, a_sem, b_ssem, b_rsem,
    kv, vt, vut, rope_t, x_ssem, x_rsem, s0_ssem, s0_rsem, s_ssem, s_rsem, y_ssem, y_rsem, o_sem,
    qf, q_snd, qg, qa, nkv, q1_ssem, q1_rsem, n1_ssem, n1_rsem, q2_ssem, q2_rsem,
    ot, ml, u_snd, u_rcv, ml_rcv, u_ssem, u_rsem, m_ssem, m_rsem,
    o_snd, o_rcv, of, hv, h_ssem, h_rsem,
):
    nz, ny, nx, half, sl, lat, heads, hs, tr, rows, steps, group, rope, scale = cfg
    wide = lat + LANES
    ctx = lax.axis_index("ctx")
    head = lax.axis_index("head")
    z, y = ctx // ny, ctx % ny
    x, c = head // CORES, head % CORES

    def dev(zz, yy, xx, cc):
        return (zz * ny + yy, xx * CORES + cc)

    def up(value, by, size):
        return (value + by) % size

    def remote(src, dst, ssem, rsem, device):
        return pltpu.make_async_remote_copy(
            src_ref=src, dst_ref=dst, send_sem=ssem, recv_sem=rsem, device_id=device, device_id_type=MESH
        )

    sibling = dev(z, y, x, 1 - c)
    x_peer = [None] + [dev(z, y, up(x, d, nx), c) for d in range(1, nx)]
    y_peer = [None] + [dev(z, up(y, d, ny), x, c) for d in range(1, ny)]

    y_order = [0, 1] + ([ny - 1] + list(range(2, ny - 1)) if ny > 2 else [])
    y_place = {d: i for i, d in enumerate(y_order)}

    loads = [
        (qn_h, qn),
        (qr_h, qr),
        (hid_h.at[pl.ds(pl.multiple_of((1 - c) * half, half), half)], hid.at[0]),
        (ld_h, ld),
        (rd_h, rd.at[pl.ds(0, rope)]),
        (hid_h.at[pl.ds(pl.multiple_of(c * half, half), half)], hid.at[1]),
        (nl_h, nl),
        (nr_h, nr),
        (gain_h, gain),
        (freq_h, freq),
        (ku_h.at[pl.ds(y * hs, hs)], ku),
        (vu_h.at[pl.ds(y * hs, hs)], vu),
    ]
    loads = [pltpu.make_async_copy(src, dst, loc.at[i]) for i, (src, dst) in enumerate(loads)]
    for load in loads:
        load.start()

    barrier = pltpu.get_barrier_semaphore()
    peers = [sibling] + x_peer[1:] + y_peer[1:] + [dev(up(z, d, nz), y, x, c) for d in range(1, nz)]
    for peer in peers:
        pl.semaphore_signal(barrier, inc=1, device_id=peer, device_id_type=MESH)

    lane = lax.broadcasted_iota(jnp.int32, (tr, LANES), 1)
    row_of = lax.broadcasted_iota(jnp.int32, (tr, LANES), 0) % rows
    request = jnp.zeros((tr, LANES), jnp.int32)
    for r in range(rows):
        request = jnp.where(row_of == r, rowreq[ctx * rows + r], request)
    one_hot = jnp.where(lane - rope == request, 1.0, 0.0)
    qf[1] = jnp.zeros(qf.shape[1:], F32)
    loads[0].wait()
    loads[1].wait()
    qf[0] = qn[...].astype(F32)
    qf[1, :, :, 0:rope] = qr[...].astype(F32)
    for h in range(heads):
        q_snd[h, :, 0:LANES] = qf[0, :, h, :].astype(BF16)
        q_snd[h, :, LANES:] = (qf[1, :, h, :] + one_hot).astype(BF16)
    qg[0, :, y] = q_snd[pl.ds(y * hs, hs)]
    loads[6].wait()
    loads[7].wait()
    nkv[y, :, 0:lat] = nl[...]
    nkv[y, :, lat:] = jnp.zeros((tr, LANES), BF16)
    nkv[y, :, lat : lat + rope] = nr[...]

    rd[pl.ds(rope, LANES - rope)] = jnp.zeros((LANES - rope, rd.shape[1]), BF16)
    for i in (2, 3, 4):
        loads[i].wait()
    a_snd[:, 0:lat] = nn(hid[0], ld[...]).astype(BF16)
    a_snd[:, lat:] = nt(hid[0], rd[...]).astype(BF16)

    pl.semaphore_wait(barrier, len(peers))
    a_copy = remote(a_snd, a_rcv, a_sem.at[0], a_sem.at[1], sibling)
    a_copy.start()
    q1, n1 = [], []
    for d in range(1, ny):
        to = up(y, d, ny)
        q1.append(
            remote(q_snd.at[pl.ds(to * hs, hs)], qg.at[0, :, y], q1_ssem.at[d], q1_rsem.at[d], y_peer[d])
        )
        n1.append(remote(nkv.at[y], nkv.at[y], n1_ssem.at[d], n1_rsem.at[d], y_peer[d]))
    for copy in q1 + n1:
        copy.start()

    loads[5].wait()
    part[:, 0:lat] = nn(hid[1], ld[...])
    part[:, lat:] = nt(hid[1], rd[...])

    for copy in q1:
        copy.wait_recv()

    def z_copy(d):
        return remote(
            qg.at[0], qg.at[d], q2_ssem.at[d], q2_rsem.at[d], dev(up(z, d, nz), y, x, c)
        )

    z_order = [(i + 1) // 2 if i % 2 else (nz - i // 2) % nz for i in range(nz)]
    for d in z_order[1:]:
        z_copy(d).start()

    a_copy.wait_recv()
    part[...] += a_rcv[...].astype(F32)
    b_snd[...] = part[...].astype(BF16).reshape(nx, sl, wide)
    b = [remote(b_snd.at[up(x, d, nx)], b_rcv.at[d], b_ssem.at[d], b_rsem.at[d], x_peer[d]) for d in range(1, nx)]
    for copy in b:
        copy.start()

    loads[11].wait()
    for h in range(hs):
        vut[pl.ds(h * LANES, LANES)] = vu[h].T
    loads[8].wait()
    loads[9].wait()
    position = (ctx * (half * CORES) + c * half + x * sl) + lax.broadcasted_iota(jnp.int32, (sl, LANES), 0)
    owner = jnp.zeros((sl, LANES), jnp.int32)
    start = jnp.zeros((sl, LANES), jnp.int32)
    end = jnp.int32(0)
    for r in range(lens.shape[0] - 1):
        end = end + lens[r]
        owner = owner + jnp.where(position >= end, 1, 0)
        start = jnp.where(position >= end, end, start)
    angle = freq[...] * (position - start).astype(F32)
    cosine, sine = jnp.cos(angle), jnp.sin(angle)
    lane = lax.broadcasted_iota(jnp.int32, (sl, LANES), 1)
    penalty = jnp.where((lane >= rope) & (lane < rope + lens.shape[0]) & (lane - rope != owner), MASKED, 0.0)

    own_rows = pl.ds(pl.multiple_of(x * sl, sl), sl)
    total = part[own_rows, :]
    for d in range(1, nx):
        b[d - 1].wait_recv()
        total = total + b_rcv[d].astype(F32)
    latent = total[:, 0:lat]
    mean_square = jnp.mean(latent * latent, axis=-1, keepdims=True)
    kv[0, 0, own_rows, 0:lat] = (latent * lax.rsqrt(mean_square + EPSILON) * gain[...]).astype(BF16)
    raw = total[:, lat:]
    turned = jnp.where(lane < rope // 2, -pltpu.roll(raw, LANES - rope // 2, 1), pltpu.roll(raw, rope // 2, 1))
    rotated = jnp.where(lane < rope, raw * cosine + turned * sine, penalty)
    kv[0, 0, own_rows, lat:] = rotated.astype(BF16)

    def x_copy(d):
        place = kv.at[0, 0, own_rows]
        return remote(place, place, x_ssem.at[d], x_rsem.at[d], x_peer[d])

    def to_sibling(d):
        part_rows = pl.ds(pl.multiple_of(up(x, nx - d, nx) * sl, sl), sl)
        return remote(kv.at[0, 0, part_rows], kv.at[1, 0, part_rows], s0_ssem.at[d], s0_rsem.at[d], sibling)

    def y_copy(d, e):
        part_rows = pl.ds(pl.multiple_of(up(x, nx - e, nx) * sl, sl), sl)
        return remote(
            kv.at[0, 0, part_rows], kv.at[0, y_place[d], part_rows], y_ssem.at[d, e], y_rsem.at[d, e], y_peer[d]
        )

    for d in range(1, nx):
        x_copy(d).start()
    to_sibling(0).start()
    for d in y_order[1:]:
        y_copy(d, 0).start()
    for e in range(1, nx):
        x_copy(e).wait_recv()
        to_sibling(e).start()
        for d in y_order[1:]:
            y_copy(d, e).start()

    ml[...] = jnp.zeros(ml.shape, F32)
    for copy in n1:
        copy.wait_recv()
    loads[10].wait()
    for e in range(nx):
        to_sibling(e).wait_recv()

    def chunk_keys(pieces):
        return jnp.concatenate([kv[i, j] for i, j in pieces], axis=0)

    def first_chunk(keys, s):
        qa[s, :, lat:] = qg[s, :, :, :, LANES:].reshape(group, LANES)
        for h in range(hs):
            qa[s, pl.ds(h * (group // hs), group // hs), 0:lat] = nn(
                qg[s, h, :, :, 0:LANES].reshape(group // hs, LANES), ku[h]
            ).astype(BF16)
        scores = nt(keys, qa[s])
        top = jnp.max(scores, axis=0, keepdims=True)
        weights = jnp.exp2((scores - top) * scale)
        ml[s, 0:1, :] = top
        ml[s, 1:2, :] = jnp.sum(weights, axis=0, keepdims=True)
        ot[s] = nn(vt[...], weights.astype(BF16))

    def next_chunk(scores, values, s):
        before = ml[s, 0:1, :]
        top = jnp.maximum(before, jnp.max(scores, axis=0, keepdims=True))
        weights = jnp.exp2((scores - top) * scale)
        keep = jnp.exp2((before - top) * scale)
        ml[s, 0:1, :] = top
        ml[s, 1:2, :] = ml[s, 1:2, :] * keep + jnp.sum(weights, axis=0, keepdims=True)
        return ot[s] * keep + nn(values, weights.astype(BF16))

    pieces = [(0, 0), (1, 0)]
    keys0 = chunk_keys(pieces)
    vt[...] = keys0[:, 0:lat].T

    def visit_first(i, carry):
        s = jnp.where(i % 2 == 1, (i + 1) // 2, (nz - i // 2) % nz)

        @pl.when(i > 0)
        def _():
            z_copy(s).wait_recv()

        first_chunk(chunk_keys([(0, 0), (1, 0)]), s)
        return carry

    lax.fori_loop(0, nz, visit_first, 0)

    sides = [c, 1 - c]
    outs = []
    for i in range(CORES):
        rope_t[i] = kv[i, 0, :, lat:].astype(F32).T[0:rope].astype(BF16)
        place = pl.ds(pl.multiple_of(sides[i] * half, half), half)
        outs.append(pltpu.make_async_copy(kv.at[i, 0, :, pl.ds(0, lat)], lat_o.at[place], o_sem.at[2 * i]))
        outs.append(pltpu.make_async_copy(rope_t.at[i], rope_o.at[:, place], o_sem.at[2 * i + 1]))
    for copy in outs:
        copy.start()

    fresh = ny * tr
    new_keys = nkv[...].reshape(fresh, wide)
    key_of = lax.broadcasted_iota(jnp.int32, (fresh, group), 0)
    query_of = lax.broadcasted_iota(jnp.int32, (fresh, group), 1) % fresh
    allowed = (
        (key_of // tr == query_of // tr)
        & (key_of % rows == query_of % rows)
        & ((key_of % tr) // rows <= (query_of % tr) // rows)
    )
    scores = jnp.where(allowed, nt(new_keys, qa[0]), MASKED)
    ot[0] = next_chunk(scores, new_keys[:, 0:lat].astype(F32).T.astype(BF16), 0)

    def arrive(p):
        for e in range(nx):
            y_copy(y_order[p], e).wait_recv()
        copy = remote(kv.at[0, p], kv.at[1, p], s_ssem.at[p], s_rsem.at[p], sibling)
        copy.start()
        return copy

    forwards = {}
    chunks = []
    if ny > 2:
        chunks = [[(0, 1), (0, 2)], [(1, 1), (1, 2)]]
    chunks += [[(0, p), (1, p)] for p in (range(3, ny) if ny > 2 else range(1, ny))]
    for number, pieces in enumerate(chunks):
        last = number == len(chunks) - 1
        for i, p in pieces:
            if p not in forwards:
                forwards[p] = arrive(p)
        for i, p in pieces:
            if i == 1:
                forwards[p].wait_recv()
        vt[...] = chunk_keys(pieces)[:, 0:lat].T
        if not last:

            def visit(i, carry, pieces=pieces):
                ot[i] = next_chunk(nt(chunk_keys(pieces), qa[i]), vt[...], i)
                return carry

            lax.fori_loop(0, nz, visit, 0)

    def lifted(s, pieces):
        mixed = next_chunk(nt(chunk_keys(pieces), qa[s]), vt[...], s).astype(BF16)
        wide_values = nn(vut[...], mixed)
        of_head = lax.broadcasted_iota(jnp.int32, (LANES, group), 1) // (group // hs)
        values = jnp.zeros((LANES, group), F32)
        for h in range(hs):
            values = jnp.where(of_head == h, wide_values[h * LANES : (h + 1) * LANES], values)
        return values

    def back(s):
        to = dev(up(z, nz - s, nz), y, x, c)
        return (
            remote(u_snd.at[s], u_rcv.at[s], u_ssem.at[s], u_rsem.at[s], to),
            remote(ml.at[s], ml_rcv.at[s], m_ssem.at[s], m_rsem.at[s], to),
        )

    def visit_last(i, carry):
        j = nz - 1 - i
        s = jnp.where(j % 2 == 1, (j + 1) // 2, (nz - j // 2) % nz)
        u_snd[s] = lifted(s, chunks[-1]).astype(BF16)
        for copy in back(s):
            copy.start()
        return carry

    lax.fori_loop(0, nz - 1, visit_last, 0)
    own_values = lifted(0, chunks[-1])

    top = ml[0, 0:1, :]
    for s in range(1, nz):
        for copy in back(s):
            copy.wait_recv()
        top = jnp.maximum(top, ml_rcv[s, 0:1, :])
    keep = jnp.exp2((ml[0, 0:1, :] - top) * scale)
    numerator = own_values * keep
    denominator = ml[0, 1:2, :] * keep
    for s in range(1, nz):
        keep = jnp.exp2((ml_rcv[s, 0:1, :] - top) * scale)
        numerator = numerator + u_rcv[s].astype(F32) * keep
        denominator = denominator + ml_rcv[s, 1:2, :] * keep
    values = (numerator / denominator).T.astype(BF16)
    o_snd[...] = values.reshape(hs, ny, tr, LANES)
    own_heads = pl.ds(y * hs, hs)
    back_y = [
        remote(o_snd.at[:, up(y, d, ny)], o_rcv.at[own_heads], h_ssem.at[d], h_rsem.at[d], y_peer[d])
        for d in range(1, ny)
    ]
    for copy in back_y:
        copy.start()
    o_rcv[own_heads] = o_snd[:, y]
    for copy in back_y:
        copy.wait_recv()
    for h in range(heads):
        of[:, h, :] = o_rcv[h].astype(F32)
    hv[...] = of[...].astype(BF16)
    hv_copy = pltpu.make_async_copy(hv, hv_o, o_sem.at[2 * CORES])
    hv_copy.start()

    a_copy.wait_send()
    for copy in q1 + n1 + b + back_y:
        copy.wait_send()
    for d in range(1, nz):
        z_copy(d).wait_send()
        for copy in back(d):
            copy.wait_send()
    for e in range(nx):
        if e:
            x_copy(e).wait_send()
        to_sibling(e).wait_send()
        for d in range(1, ny):
            y_copy(d, e).wait_send()
    for copy in forwards.values():
        copy.wait_send()
    for copy in outs:
        copy.wait()
    hv_copy.wait()


def local(
    prompt_hidden,
    latent_down,
    rope_down,
    latent_gain,
    request_lengths,
    row_request,
    query_nope,
    query_rope,
    new_latent,
    new_rope,
    key_up,
    value_up,
):
    ny = Y_SIZE
    nz = lax.axis_size("ctx") // ny
    nx = lax.axis_size("head") // CORES
    tok, depth = prompt_hidden.shape
    half = tok // CORES
    sl = half // nx
    steps, rows, heads, nope = query_nope.shape
    rope = query_rope.shape[-1]
    lat = key_up.shape[-1]
    tr = steps * rows
    hs = heads // ny
    group = hs * ny * tr
    wide = lat + LANES
    scale = math.log2(math.e) / math.sqrt(nope + rope)
    cfg = (nz, ny, nx, half, sl, lat, heads, hs, tr, rows, steps, group, rope, scale)
    spare = np.zeros((1, LANES), np.float32)
    frequency = 10000.0 ** (-2.0 * np.arange(rope // 2, dtype=np.float32) / rope)
    spare[0, :rope] = np.tile(frequency.astype(np.float32), 2)
    dma = pltpu.SemaphoreType.DMA
    vmem = pltpu.VMEM
    scratch = [
        vmem((2, half, depth), BF16),
        vmem((depth, lat), BF16),
        vmem((LANES, depth), BF16),
        vmem((1, lat), F32),
        vmem((tr, heads, nope), BF16),
        vmem((tr, heads, rope), BF16),
        vmem((tr, lat), BF16),
        vmem((tr, rope), BF16),
        vmem((hs, nope, lat), BF16),
        vmem((hs, lat, LANES), BF16),
        vmem((1, LANES), F32),
        dma((12,)),
        vmem((half, wide), BF16),
        vmem((half, wide), BF16),
        vmem((half, wide), F32),
        vmem((nx, sl, wide), BF16),
        vmem((nx, sl, wide), BF16),
        dma((2,)),
        dma((nx,)),
        dma((nx,)),
        vmem((CORES, ny, half, wide), BF16),
        vmem((lat, tok), BF16),
        vmem((hs * LANES, lat), BF16),
        vmem((CORES, rope, half), BF16),
        dma((nx,)),
        dma((nx,)),
        dma((nx,)),
        dma((nx,)),
        dma((ny,)),
        dma((ny,)),
        dma((ny, nx)),
        dma((ny, nx)),
        dma((2 * CORES + 1,)),
        vmem((2, tr, heads, LANES), F32),
        vmem((heads, tr, 2 * LANES), BF16),
        vmem((nz, hs, ny, tr, 2 * LANES), BF16),
        vmem((nz, group, wide), BF16),
        vmem((ny, tr, wide), BF16),
        dma((ny,)),
        dma((ny,)),
        dma((ny,)),
        dma((ny,)),
        dma((nz,)),
        dma((nz,)),
        vmem((nz, lat, group), F32),
        vmem((nz, 8, group), F32),
        vmem((nz, LANES, group), BF16),
        vmem((nz, LANES, group), BF16),
        vmem((nz, 8, group), F32),
        dma((nz,)),
        dma((nz,)),
        dma((nz,)),
        dma((nz,)),
        vmem((hs, ny, tr, LANES), BF16),
        vmem((heads, tr, LANES), BF16),
        vmem((tr, heads, LANES), F32),
        vmem((tr, heads, LANES), BF16),
        dma((ny,)),
        dma((ny,)),
    ]
    anywhere = pl.BlockSpec(memory_space=pl.ANY)
    scalars = pl.BlockSpec(memory_space=pltpu.SMEM)
    latent_cache, rope_cache, head_values = pl.pallas_call(
        functools.partial(kernel, cfg),
        out_shape=(
            jax.ShapeDtypeStruct((tok, lat), BF16),
            jax.ShapeDtypeStruct((rope, tok), BF16),
            jax.ShapeDtypeStruct((tr, heads, LANES), BF16),
        ),
        in_specs=[anywhere] * 4 + [scalars] * 2 + [anywhere] * 7,
        out_specs=(anywhere,) * 3,
        scratch_shapes=scratch,
        compiler_params=pltpu.CompilerParams(
            collective_id=0, has_side_effects=True, vmem_limit_bytes=50 * 1024 * 1024
        ),
    )(
        prompt_hidden,
        latent_down,
        rope_down,
        latent_gain.reshape(1, lat),
        request_lengths,
        row_request,
        query_nope.reshape(tr, heads, nope),
        query_rope.reshape(tr, heads, rope),
        new_latent.reshape(tr, lat),
        new_rope.reshape(tr, rope),
        key_up,
        value_up,
        jnp.asarray(spare),
    )
    return (latent_cache, rope_cache, head_values.reshape(steps, rows, heads, LANES))


def solution(mesh):
    placed = (
        P("ctx", "head"),
        P("head", None),
        P(None, "head"),
        P(),
        P(),
        P(),
        P(None, "ctx", "head", None),
        P(None, "ctx", "head", None),
        P(None, "ctx", None),
        P(None, "ctx", None),
        P("head", None, None),
        P("head", None, None),
    )
    return jax.shard_map(
        local,
        mesh=mesh,
        in_specs=placed,
        out_specs=(P("ctx", None), P(None, "ctx"), P(None, "ctx", "head", None)),
        check_vma=False,
    )
```

```python
import functools
import math

import jax
import jax.numpy as jnp
import numpy as np
from jax import lax
from jax.experimental import pallas as pl
from jax.experimental.pallas import tpu as pltpu
from jax.sharding import PartitionSpec as P

MESH = pl.DeviceIdType.MESH
EPSILON = 1e-6
MASKED = -1e30
Y_SIZE = 4
CORES = 2
LANES = 128
AT_ONCE = 4
F32 = jnp.float32
BF16 = jnp.bfloat16


def nt(a, b):
    return lax.dot_general(a, b, (((1,), (1,)), ((), ())), preferred_element_type=F32)


def nn(a, b):
    return jnp.dot(a, b, preferred_element_type=F32)


def kernel(
    cfg,
    hid_h, ld_h, rd_h, gain_h, lens, rowreq, qn_h, qr_h, nl_h, nr_h, ku_h, vu_h, freq_h,
    lat_o, rope_o, hv_o,
    hid, ld, rd, gain, qn, qr, nl, nr, ku, vu, freq, loc,
    a_snd, a_rcv, part, b_snd, b_rcv, a_sem, b_ssem, b_rsem,
    kv, vt, vut, rope_t, x_ssem, x_rsem, s0_ssem, s0_rsem, s_ssem, s_rsem, y_ssem, y_rsem, o_sem,
    qf, q_snd, qg, qa, nkv, q1_ssem, q1_rsem, n1_ssem, n1_rsem, q2_ssem, q2_rsem,
    ot, ml, u_snd, u_rcv, ml_rcv, u_ssem, u_rsem, m_ssem, m_rsem,
    o_snd, o_rcv, of, hv, h_ssem, h_rsem,
):
    nz, ny, nx, half, sl, lat, heads, hs, tr, rows, steps, group, rope, scale = cfg
    wide = lat + LANES
    ctx = lax.axis_index("ctx")
    head = lax.axis_index("head")
    z, y = ctx // ny, ctx % ny
    x, c = head // CORES, head % CORES

    def dev(zz, yy, xx, cc):
        return (zz * ny + yy, xx * CORES + cc)

    def up(value, by, size):
        return (value + by) % size

    def remote(src, dst, ssem, rsem, device):
        return pltpu.make_async_remote_copy(
            src_ref=src, dst_ref=dst, send_sem=ssem, recv_sem=rsem, device_id=device, device_id_type=MESH
        )

    sibling = dev(z, y, x, 1 - c)
    x_peer = [None] + [dev(z, y, up(x, d, nx), c) for d in range(1, nx)]
    y_peer = [None] + [dev(z, up(y, d, ny), x, c) for d in range(1, ny)]

    y_order = [0, 1] + ([ny - 1] + list(range(2, ny - 1)) if ny > 2 else [])
    y_place = {d: i for i, d in enumerate(y_order)}

    loads = [
        (qn_h, qn),
        (qr_h, qr),
        (hid_h.at[pl.ds(pl.multiple_of((1 - c) * half, half), half)], hid.at[0]),
        (ld_h, ld),
        (rd_h, rd.at[pl.ds(0, rope)]),
        (hid_h.at[pl.ds(pl.multiple_of(c * half, half), half)], hid.at[1]),
        (nl_h, nl),
        (nr_h, nr),
        (gain_h, gain),
        (freq_h, freq),
        (ku_h.at[pl.ds(y * hs, hs)], ku),
        (vu_h.at[pl.ds(y * hs, hs)], vu),
    ]
    loads = [pltpu.make_async_copy(src, dst, loc.at[i]) for i, (src, dst) in enumerate(loads)]
    for load in loads:
        load.start()

    barrier = pltpu.get_barrier_semaphore()
    peers = [sibling] + x_peer[1:] + y_peer[1:] + [dev(up(z, d, nz), y, x, c) for d in range(1, nz)]
    for peer in peers:
        pl.semaphore_signal(barrier, inc=1, device_id=peer, device_id_type=MESH)

    lane = lax.broadcasted_iota(jnp.int32, (tr, LANES), 1)
    row_of = lax.broadcasted_iota(jnp.int32, (tr, LANES), 0) % rows
    request = jnp.zeros((tr, LANES), jnp.int32)
    for r in range(rows):
        request = jnp.where(row_of == r, rowreq[ctx * rows + r], request)
    one_hot = jnp.where(lane - rope == request, 1.0, 0.0)
    qf[1] = jnp.zeros(qf.shape[1:], F32)
    loads[0].wait()
    loads[1].wait()
    qf[0] = qn[...].astype(F32)
    qf[1, :, :, 0:rope] = qr[...].astype(F32)
    for h in range(heads):
        q_snd[h, :, 0:LANES] = qf[0, :, h, :].astype(BF16)
        q_snd[h, :, LANES:] = (qf[1, :, h, :] + one_hot).astype(BF16)
    qg[0, :, y] = q_snd[pl.ds(y * hs, hs)]
    loads[6].wait()
    loads[7].wait()
    nkv[y, :, 0:lat] = nl[...].reshape(tr, lat)
    nkv[y, :, lat:] = jnp.zeros((tr, LANES), BF16)
    nkv[y, :, lat : lat + rope] = nr[...].reshape(tr, rope)

    rd[pl.ds(rope, LANES - rope)] = jnp.zeros((LANES - rope, rd.shape[1]), BF16)
    for i in (2, 3, 4):
        loads[i].wait()
    a_snd[:, 0:lat] = nn(hid[0], ld[...]).astype(BF16)
    a_snd[:, lat:] = nt(hid[0], rd[...]).astype(BF16)

    pl.semaphore_wait(barrier, len(peers))
    a_copy = remote(a_snd, a_rcv, a_sem.at[0], a_sem.at[1], sibling)
    a_copy.start()
    q1, n1 = [], []
    for d in range(1, ny):
        to = up(y, d, ny)
        q1.append(
            remote(q_snd.at[pl.ds(to * hs, hs)], qg.at[0, :, y], q1_ssem.at[d], q1_rsem.at[d], y_peer[d])
        )
        n1.append(remote(nkv.at[y], nkv.at[y], n1_ssem.at[d], n1_rsem.at[d], y_peer[d]))
    for copy in q1 + n1:
        copy.start()

    loads[5].wait()
    part[:, 0:lat] = nn(hid[1], ld[...])
    part[:, lat:] = nt(hid[1], rd[...])

    for copy in q1:
        copy.wait_recv()

    def z_copy(d):
        return remote(
            qg.at[0], qg.at[d], q2_ssem.at[d], q2_rsem.at[d], dev(up(z, d, nz), y, x, c)
        )

    z_order = [(i + 1) // 2 if i % 2 else (nz - i // 2) % nz for i in range(nz)]
    for d in z_order[1:]:
        z_copy(d).start()

    a_copy.wait_recv()
    part[...] += a_rcv[...].astype(F32)
    b_snd[...] = part[...].astype(BF16).reshape(nx, sl, wide)
    b = [remote(b_snd.at[up(x, d, nx)], b_rcv.at[d], b_ssem.at[d], b_rsem.at[d], x_peer[d]) for d in range(1, nx)]
    for copy in b:
        copy.start()

    loads[11].wait()
    for h in range(hs):
        vut[pl.ds(h * LANES, LANES)] = vu[h].T
    loads[8].wait()
    loads[9].wait()
    position = (ctx * (half * CORES) + c * half + x * sl) + lax.broadcasted_iota(jnp.int32, (sl, LANES), 0)
    owner = jnp.zeros((sl, LANES), jnp.int32)
    start = jnp.zeros((sl, LANES), jnp.int32)
    end = jnp.int32(0)
    for r in range(lens.shape[0] - 1):
        end = end + lens[r]
        owner = owner + jnp.where(position >= end, 1, 0)
        start = jnp.where(position >= end, end, start)
    angle = freq[...] * (position - start).astype(F32)
    cosine, sine = jnp.cos(angle), jnp.sin(angle)
    lane = lax.broadcasted_iota(jnp.int32, (sl, LANES), 1)
    penalty = jnp.where((lane >= rope) & (lane < rope + lens.shape[0]) & (lane - rope != owner), MASKED, 0.0)

    own_rows = pl.ds(pl.multiple_of(x * sl, sl), sl)
    total = part[own_rows, :]
    for d in range(1, nx):
        b[d - 1].wait_recv()
        total = total + b_rcv[d].astype(F32)
    latent = total[:, 0:lat]
    mean_square = jnp.mean(latent * latent, axis=-1, keepdims=True)
    kv[0, 0, own_rows, 0:lat] = (latent * lax.rsqrt(mean_square + EPSILON) * gain[...]).astype(BF16)
    raw = total[:, lat:]
    turned = jnp.where(lane < rope // 2, -pltpu.roll(raw, LANES - rope // 2, 1), pltpu.roll(raw, rope // 2, 1))
    rotated = jnp.where(lane < rope, raw * cosine + turned * sine, penalty)
    kv[0, 0, own_rows, lat:] = rotated.astype(BF16)

    def x_copy(d):
        place = kv.at[0, 0, own_rows]
        return remote(place, place, x_ssem.at[d], x_rsem.at[d], x_peer[d])

    def to_sibling(d):
        part_rows = pl.ds(pl.multiple_of(up(x, nx - d, nx) * sl, sl), sl)
        return remote(kv.at[0, 0, part_rows], kv.at[1, 0, part_rows], s0_ssem.at[d], s0_rsem.at[d], sibling)

    def y_copy(d, e):
        part_rows = pl.ds(pl.multiple_of(up(x, nx - e, nx) * sl, sl), sl)
        return remote(
            kv.at[0, 0, part_rows], kv.at[0, y_place[d], part_rows], y_ssem.at[d, e], y_rsem.at[d, e], y_peer[d]
        )

    for d in range(1, nx):
        x_copy(d).start()
    to_sibling(0).start()
    for d in y_order[1:]:
        y_copy(d, 0).start()
    for e in range(1, nx):
        x_copy(e).wait_recv()
        to_sibling(e).start()
        for d in y_order[1:]:
            y_copy(d, e).start()

    ml[...] = jnp.zeros(ml.shape, F32)
    for copy in n1:
        copy.wait_recv()
    loads[10].wait()
    for e in range(nx):
        to_sibling(e).wait_recv()

    def chunk_keys(pieces):
        return jnp.concatenate([kv[i, j] for i, j in pieces], axis=0)

    def transpose_values(pieces):
        for k, (i, j) in enumerate(pieces):
            vt[:, k * half : (k + 1) * half] = kv[i, j, :, 0:lat].T

    def absorb(s):
        qa[s, :, lat:] = qg[s, :, :, :, LANES:].reshape(group, LANES)
        for h in range(hs):
            qa[s, pl.ds(h * (group // hs), group // hs), 0:lat] = nn(
                qg[s, h, :, :, 0:LANES].reshape(group // hs, LANES), ku[h]
            ).astype(BF16)

    def first_keys(keys, values, slots):
        scores = [nt(keys, qa[s]) for s in slots]
        tops = [jnp.max(score, axis=0, keepdims=True) for score in scores]
        weights = [jnp.exp2((score - top) * scale) for score, top in zip(scores, tops)]
        sums = [jnp.sum(weight, axis=0, keepdims=True) for weight in weights]
        mixed = [nn(values, weight.astype(BF16)) for weight in weights]
        return tops, sums, mixed

    def next_keys(scores, values, slots):
        before = [ml[s, 0:1, :] for s in slots]
        sums = [ml[s, 1:2, :] for s in slots]
        tops = [jnp.maximum(old, jnp.max(score, axis=0, keepdims=True)) for old, score in zip(before, scores)]
        weights = [jnp.exp2((score - top) * scale) for score, top in zip(scores, tops)]
        keeps = [jnp.exp2((old - top) * scale) for old, top in zip(before, tops)]
        sums = [
            old * keep + jnp.sum(weight, axis=0, keepdims=True) for old, keep, weight in zip(sums, keeps, weights)
        ]
        mixed = [
            ot[s] * keep + nn(values, weight.astype(BF16)) for s, keep, weight in zip(slots, keeps, weights)
        ]
        return tops, sums, mixed

    def put(slots, tops, sums, mixed):
        for s, top, total, mix in zip(slots, tops, sums, mixed):
            ml[s, 0:1, :] = top
            ml[s, 1:2, :] = total
            if mix is not None:
                ot[s] = mix

    at_once = min(AT_ONCE, nz)
    bunches = [z_order[i : i + at_once] for i in range(0, nz, at_once)]
    own_pieces = [(0, 0), (1, 0)]
    transpose_values(own_pieces)
    for slots in bunches:
        for s in slots:
            if s:
                z_copy(s).wait_recv()
            absorb(s)
        put(slots, *first_keys(chunk_keys(own_pieces), vt[:, 0 : CORES * half], slots))

    sides = [c, 1 - c]
    outs = []
    for i in range(CORES):
        rope_t[i] = kv[i, 0, :, lat:].astype(F32).T[0:rope].astype(BF16)
        place = pl.ds(pl.multiple_of(sides[i] * half, half), half)
        outs.append(pltpu.make_async_copy(kv.at[i, 0, :, pl.ds(0, lat)], lat_o.at[place], o_sem.at[2 * i]))
        outs.append(pltpu.make_async_copy(rope_t.at[i], rope_o.at[:, place], o_sem.at[2 * i + 1]))
    for copy in outs:
        copy.start()

    fresh = ny * tr
    new_keys = nkv[...].reshape(fresh, wide)
    key_of = lax.broadcasted_iota(jnp.int32, (fresh, group), 0)
    query_of = lax.broadcasted_iota(jnp.int32, (fresh, group), 1) % fresh
    allowed = (
        (key_of // tr == query_of // tr)
        & (key_of % rows == query_of % rows)
        & ((key_of % tr) // rows <= (query_of % tr) // rows)
    )
    scores = jnp.where(allowed, nt(new_keys, qa[0]), MASKED)
    put([0], *next_keys([scores], new_keys[:, 0:lat].astype(F32).T.astype(BF16), [0]))

    def arrive(p):
        for e in range(nx):
            y_copy(y_order[p], e).wait_recv()
        copy = remote(kv.at[0, p], kv.at[1, p], s_ssem.at[p], s_rsem.at[p], sibling)
        copy.start()
        return copy

    forwards = {}
    chunks = []
    if ny > 2:
        chunks = [[(0, 1), (0, 2), (1, 1), (1, 2)]]
    chunks += [[(0, p), (1, p)] for p in (range(3, ny) if ny > 2 else range(1, ny))]
    for pieces in chunks[:-1]:
        for i, p in pieces:
            if p not in forwards:
                forwards[p] = arrive(p)
        for i, p in pieces:
            if i == 1:
                forwards[p].wait_recv()
        transpose_values(pieces)
        for slots in bunches:
            keys = chunk_keys(pieces)
            put(slots, *next_keys([nt(keys, qa[s]) for s in slots], vt[:, 0 : len(pieces) * half], slots))

    def back(s):
        to = dev(up(z, nz - s, nz), y, x, c)
        return (
            remote(u_snd.at[s], u_rcv.at[s], u_ssem.at[s], u_rsem.at[s], to),
            remote(ml.at[s], ml_rcv.at[s], m_ssem.at[s], m_rsem.at[s], to),
        )

    pieces = chunks[-1]
    for i, p in pieces:
        if p not in forwards:
            forwards[p] = arrive(p)
    for i, p in pieces:
        if i == 1:
            forwards[p].wait_recv()
    transpose_values(pieces)
    of_head = lax.broadcasted_iota(jnp.int32, (LANES, group), 1) // (group // hs)
    own_values = None
    for slots in bunches[::-1]:
        slots = slots[::-1]
        keys = chunk_keys(pieces)
        tops, sums, mixed = next_keys([nt(keys, qa[s]) for s in slots], vt[:, 0 : len(pieces) * half], slots)
        put(slots, tops, sums, [None] * len(slots))
        for s, mix in zip(slots, mixed):
            every = nn(vut[...], mix.astype(BF16))
            values = every[0:LANES]
            for h in range(1, hs):
                values = jnp.where(of_head == h, every[h * LANES : (h + 1) * LANES], values)
            if s:
                u_snd[s] = values.astype(BF16)
            else:
                own_values = values
        for s in slots:
            if s:
                for copy in back(s):
                    copy.start()

    top = ml[0, 0:1, :]
    for s in range(1, nz):
        for copy in back(s):
            copy.wait_recv()
        top = jnp.maximum(top, ml_rcv[s, 0:1, :])
    keep = jnp.exp2((ml[0, 0:1, :] - top) * scale)
    numerator = own_values * keep
    denominator = ml[0, 1:2, :] * keep
    for s in range(1, nz):
        keep = jnp.exp2((ml_rcv[s, 0:1, :] - top) * scale)
        numerator = numerator + u_rcv[s].astype(F32) * keep
        denominator = denominator + ml_rcv[s, 1:2, :] * keep
    values = (numerator / denominator).T.astype(BF16)
    o_snd[...] = values.reshape(hs, ny, tr, LANES)
    own_heads = pl.ds(y * hs, hs)
    back_y = [
        remote(o_snd.at[:, up(y, d, ny)], o_rcv.at[own_heads], h_ssem.at[d], h_rsem.at[d], y_peer[d])
        for d in range(1, ny)
    ]
    for copy in back_y:
        copy.start()
    o_rcv[own_heads] = o_snd[:, y]
    for copy in back_y:
        copy.wait_recv()
    for h in range(heads):
        of[:, h, :] = o_rcv[h].astype(F32)
    hv[...] = of[...].astype(BF16)
    hv_copy = pltpu.make_async_copy(hv, hv_o, o_sem.at[2 * CORES])
    hv_copy.start()

    a_copy.wait_send()
    for copy in q1 + n1 + b + back_y:
        copy.wait_send()
    for d in range(1, nz):
        z_copy(d).wait_send()
        for copy in back(d):
            copy.wait_send()
    for e in range(nx):
        if e:
            x_copy(e).wait_send()
        to_sibling(e).wait_send()
        for d in range(1, ny):
            y_copy(d, e).wait_send()
    for copy in forwards.values():
        copy.wait_send()
    for copy in outs:
        copy.wait()
    hv_copy.wait()


def local(
    prompt_hidden,
    latent_down,
    rope_down,
    latent_gain,
    request_lengths,
    row_request,
    query_nope,
    query_rope,
    new_latent,
    new_rope,
    key_up,
    value_up,
):
    ny = Y_SIZE
    nz = lax.axis_size("ctx") // ny
    nx = lax.axis_size("head") // CORES
    tok, depth = prompt_hidden.shape
    half = tok // CORES
    sl = half // nx
    steps, rows, heads, nope = query_nope.shape
    rope = query_rope.shape[-1]
    lat = key_up.shape[-1]
    tr = steps * rows
    hs = heads // ny
    group = hs * ny * tr
    wide = lat + LANES
    scale = math.log2(math.e) / math.sqrt(nope + rope)
    cfg = (nz, ny, nx, half, sl, lat, heads, hs, tr, rows, steps, group, rope, scale)
    spare = np.zeros((1, LANES), np.float32)
    frequency = 10000.0 ** (-2.0 * np.arange(rope // 2, dtype=np.float32) / rope)
    spare[0, :rope] = np.tile(frequency.astype(np.float32), 2)
    dma = pltpu.SemaphoreType.DMA
    vmem = pltpu.VMEM
    scratch = [
        vmem((2, half, depth), BF16),
        vmem((depth, lat), BF16),
        vmem((LANES, depth), BF16),
        vmem((1, lat), F32),
        vmem((tr, heads, nope), BF16),
        vmem((tr, heads, rope), BF16),
        vmem((steps, rows, lat), BF16),
        vmem((steps, rows, rope), BF16),
        vmem((hs, nope, lat), BF16),
        vmem((hs, lat, LANES), BF16),
        vmem((1, LANES), F32),
        dma((12,)),
        vmem((half, wide), BF16),
        vmem((half, wide), BF16),
        vmem((half, wide), F32),
        vmem((nx, sl, wide), BF16),
        vmem((nx, sl, wide), BF16),
        dma((2,)),
        dma((nx,)),
        dma((nx,)),
        vmem((CORES, ny, half, wide), BF16),
        vmem((lat, max(1, ny // 2) * tok), BF16),
        vmem((hs * LANES, lat), BF16),
        vmem((CORES, rope, half), BF16),
        dma((nx,)),
        dma((nx,)),
        dma((nx,)),
        dma((nx,)),
        dma((ny,)),
        dma((ny,)),
        dma((ny, nx)),
        dma((ny, nx)),
        dma((2 * CORES + 1,)),
        vmem((2, tr, heads, LANES), F32),
        vmem((heads, tr, 2 * LANES), BF16),
        vmem((nz, hs, ny, tr, 2 * LANES), BF16),
        vmem((nz, group, wide), BF16),
        vmem((ny, tr, wide), BF16),
        dma((ny,)),
        dma((ny,)),
        dma((ny,)),
        dma((ny,)),
        dma((nz,)),
        dma((nz,)),
        vmem((nz, lat, group), F32),
        vmem((nz, 8, group), F32),
        vmem((nz, LANES, group), BF16),
        vmem((nz, LANES, group), BF16),
        vmem((nz, 8, group), F32),
        dma((nz,)),
        dma((nz,)),
        dma((nz,)),
        dma((nz,)),
        vmem((hs, ny, tr, LANES), BF16),
        vmem((heads, tr, LANES), BF16),
        vmem((tr, heads, LANES), F32),
        vmem((tr, heads, LANES), BF16),
        dma((ny,)),
        dma((ny,)),
    ]
    anywhere = pl.BlockSpec(memory_space=pl.ANY)
    scalars = pl.BlockSpec(memory_space=pltpu.SMEM)
    latent_cache, rope_cache, head_values = pl.pallas_call(
        functools.partial(kernel, cfg),
        out_shape=(
            jax.ShapeDtypeStruct((tok, lat), BF16),
            jax.ShapeDtypeStruct((rope, tok), BF16),
            jax.ShapeDtypeStruct((tr, heads, LANES), BF16),
        ),
        in_specs=[anywhere] * 4 + [scalars] * 2 + [anywhere] * 7,
        out_specs=(anywhere,) * 3,
        scratch_shapes=scratch,
        compiler_params=pltpu.CompilerParams(
            collective_id=0, has_side_effects=True, vmem_limit_bytes=60 * 1024 * 1024
        ),
    )(
        prompt_hidden,
        latent_down,
        rope_down,
        latent_gain.reshape(1, lat),
        request_lengths,
        row_request,
        query_nope.reshape(tr, heads, nope),
        query_rope.reshape(tr, heads, rope),
        new_latent,
        new_rope,
        key_up,
        value_up,
        jnp.asarray(spare),
    )
    return (latent_cache, rope_cache, head_values.reshape(steps, rows, heads, LANES))


def solution(mesh):
    placed = (
        P("ctx", "head"),
        P("head", None),
        P(None, "head"),
        P(),
        P(),
        P(),
        P(None, "ctx", "head", None),
        P(None, "ctx", "head", None),
        P(None, "ctx", None),
        P(None, "ctx", None),
        P("head", None, None),
        P("head", None, None),
    )
    return jax.shard_map(
        local,
        mesh=mesh,
        in_specs=placed,
        out_specs=(P("ctx", None), P(None, "ctx"), P(None, "ctx", "head", None)),
        check_vma=False,
    )
```

```python
import functools
import math

import jax
import jax.numpy as jnp
import numpy as np
from jax import lax
from jax.experimental import pallas as pl
from jax.experimental.pallas import tpu as pltpu
from jax.sharding import PartitionSpec as P

MESH = pl.DeviceIdType.MESH
EPSILON = 1e-6
MASKED = -1e30
Y_SIZE = 4
CORES = 2
LANES = 128
LAST_AT_ONCE = 2
AT_ONCE = 4
F32 = jnp.float32
BF16 = jnp.bfloat16


def nt(a, b):
    return lax.dot_general(a, b, (((1,), (1,)), ((), ())), preferred_element_type=F32)


def nn(a, b):
    return jnp.dot(a, b, preferred_element_type=F32)


def kernel(
    cfg,
    hid_h, ld_h, rd_h, gain_h, lens, rowreq, qn_h, qr_h, nl_h, nr_h, ku_h, vu_h, freq_h,
    lat_o, rope_o, hv_o,
    hid, ld, rd, gain, qn, qr, nl, nr, ku, vu, freq, loc,
    a_snd, a_rcv, part, b_snd, b_rcv, a_sem, b_ssem, b_rsem,
    kv, vt, vut, rope_t, x_ssem, x_rsem, s0_ssem, s0_rsem, s_ssem, s_rsem, y_ssem, y_rsem, o_sem,
    qf, q_snd, qg, qa, nkv, q1_ssem, q1_rsem, n1_ssem, n1_rsem, q2_ssem, q2_rsem,
    ot, ml, u_snd, u_rcv, ml_rcv, u_ssem, u_rsem, m_ssem, m_rsem,
    o_snd, o_rcv, of, hv, h_ssem, h_rsem,
):
    nz, ny, nx, half, sl, lat, heads, hs, tr, rows, steps, group, rope, scale = cfg
    wide = lat + LANES
    ctx = lax.axis_index("ctx")
    head = lax.axis_index("head")
    z, y = ctx // ny, ctx % ny
    x, c = head // CORES, head % CORES

    def dev(zz, yy, xx, cc):
        return (zz * ny + yy, xx * CORES + cc)

    def up(value, by, size):
        return (value + by) % size

    def remote(src, dst, ssem, rsem, device):
        return pltpu.make_async_remote_copy(
            src_ref=src, dst_ref=dst, send_sem=ssem, recv_sem=rsem, device_id=device, device_id_type=MESH
        )

    sibling = dev(z, y, x, 1 - c)
    x_peer = [None] + [dev(z, y, up(x, d, nx), c) for d in range(1, nx)]
    y_peer = [None] + [dev(z, up(y, d, ny), x, c) for d in range(1, ny)]

    y_order = [0, 1] + ([ny - 1] + list(range(2, ny - 1)) if ny > 2 else [])
    y_place = {d: i for i, d in enumerate(y_order)}
    y_near = y_order[1:3]
    y_far = y_order[3:]

    loads = [
        (qn_h, qn),
        (qr_h, qr),
        (hid_h.at[pl.ds(pl.multiple_of((1 - c) * half, half), half)], hid.at[0]),
        (ld_h, ld),
        (rd_h, rd.at[pl.ds(0, rope)]),
        (hid_h.at[pl.ds(pl.multiple_of(c * half, half), half)], hid.at[1]),
        (nl_h, nl),
        (nr_h, nr),
        (gain_h, gain),
        (freq_h, freq),
        (ku_h.at[pl.ds(y * hs, hs)], ku),
        (vu_h.at[pl.ds(y * hs, hs)], vu),
    ]
    loads = [pltpu.make_async_copy(src, dst, loc.at[i]) for i, (src, dst) in enumerate(loads)]
    for load in loads:
        load.start()

    barrier = pltpu.get_barrier_semaphore()
    peers = [sibling] + x_peer[1:] + y_peer[1:] + [dev(up(z, d, nz), y, x, c) for d in range(1, nz)]
    for peer in peers:
        pl.semaphore_signal(barrier, inc=1, device_id=peer, device_id_type=MESH)

    loads[0].wait()
    loads[1].wait()
    qf[0] = qn[...].astype(F32)
    qf[1, :, :, 0:rope] = qr[...].astype(F32)
    lane = lax.broadcasted_iota(jnp.int32, (tr, LANES), 1)
    for h in range(heads):
        q_snd[h // hs, h % hs] = qf[0, :, h, :].astype(BF16)
    for h in range(0, heads, 2):
        pair = jnp.where(lane < rope, qf[1, :, h, :], pltpu.roll(qf[1, :, h + 1, :], rope, 1))
        q_snd[h // hs, hs + (h % hs) // 2] = pair.astype(BF16)
    qg[0, :, y] = q_snd[y]
    loads[6].wait()
    loads[7].wait()
    nkv[y, :, 0:lat] = nl[...].reshape(tr, lat)
    nkv[y, :, lat:] = jnp.zeros((tr, LANES), BF16)
    nkv[y, :, lat : lat + rope] = nr[...].reshape(tr, rope)

    rd[pl.ds(rope, LANES - rope)] = jnp.zeros((LANES - rope, rd.shape[1]), BF16)
    for i in (2, 3, 4):
        loads[i].wait()
    a_snd[:, 0:lat] = nn(hid[0], ld[...]).astype(BF16)
    a_snd[:, lat:] = nt(hid[0], rd[...]).astype(BF16)

    pl.semaphore_wait(barrier, len(peers))
    a_copy = remote(a_snd, a_rcv, a_sem.at[0], a_sem.at[1], sibling)
    a_copy.start()
    q1, n1 = [], []
    for d in range(1, ny):
        to = up(y, d, ny)
        q1.append(
            remote(q_snd.at[to], qg.at[0, :, y], q1_ssem.at[d], q1_rsem.at[d], y_peer[d])
        )
        n1.append(remote(nkv.at[y], nkv.at[y], n1_ssem.at[d], n1_rsem.at[d], y_peer[d]))
    for copy in q1 + n1:
        copy.start()

    loads[5].wait()
    part[:, 0:lat] = nn(hid[1], ld[...])
    part[:, lat:] = nt(hid[1], rd[...])

    for copy in q1:
        copy.wait_recv()

    def z_copies(step):
        forth = remote(
            qg.at[step - 1], qg.at[step], q2_ssem.at[0, step], q2_rsem.at[0, step], dev(up(z, 1, nz), y, x, c)
        )
        back_slot = (nz - step + 1) % nz
        back = remote(
            qg.at[back_slot],
            qg.at[nz - step],
            q2_ssem.at[1, step],
            q2_rsem.at[1, step],
            dev(up(z, nz - 1, nz), y, x, c),
        )
        return forth, back

    z_far = None
    if nz > 1:
        z_far = remote(
            qg.at[0],
            qg.at[nz // 2],
            q2_ssem.at[0, nz // 2],
            q2_rsem.at[0, nz // 2],
            dev(up(z, nz // 2, nz), y, x, c),
        )
    z_steps = {step: z_copies(step) for step in range(1, nz // 2)}
    z_received = set()

    def z_receive(step):
        if step in z_steps and step not in z_received:
            z_received.add(step)
            for copy in z_steps[step]:
                copy.wait_recv()

    def z_send(step):
        if step in z_steps:
            for copy in z_steps[step]:
                copy.start()

    z_order = [(i + 1) // 2 if i % 2 else (nz - i // 2) % nz for i in range(nz)]
    z_send(1)

    a_copy.wait_recv()
    part[...] += a_rcv[...].astype(F32)
    b_snd[...] = part[...].astype(BF16).reshape(nx, sl, wide)
    b = [remote(b_snd.at[up(x, d, nx)], b_rcv.at[d], b_ssem.at[d], b_rsem.at[d], x_peer[d]) for d in range(1, nx)]
    for copy in b:
        copy.start()
    z_receive(1)
    z_send(2)
    if z_far is not None:
        z_far.start()

    loads[11].wait()
    for h in range(hs):
        vut[pl.ds(h * LANES, LANES)] = vu[h].T
    loads[8].wait()
    loads[9].wait()
    position = (ctx * (half * CORES) + c * half + x * sl) + lax.broadcasted_iota(jnp.int32, (sl, LANES), 0)
    owner = jnp.zeros((sl, LANES), jnp.int32)
    start = jnp.zeros((sl, LANES), jnp.int32)
    end = jnp.int32(0)
    for r in range(lens.shape[0] - 1):
        end = end + lens[r]
        owner = owner + jnp.where(position >= end, 1, 0)
        start = jnp.where(position >= end, end, start)
    angle = freq[...] * (position - start).astype(F32)
    cosine, sine = jnp.cos(angle), jnp.sin(angle)
    lane = lax.broadcasted_iota(jnp.int32, (sl, LANES), 1)
    penalty = jnp.where((lane >= rope) & (lane < rope + lens.shape[0]) & (lane - rope != owner), MASKED, 0.0)

    own_rows = pl.ds(pl.multiple_of(x * sl, sl), sl)
    total = part[own_rows, :]
    for d in range(1, nx):
        b[d - 1].wait_recv()
        total = total + b_rcv[d].astype(F32)
    latent = total[:, 0:lat]
    mean_square = jnp.mean(latent * latent, axis=-1, keepdims=True)
    kv[0, 0, own_rows, 0:lat] = (latent * lax.rsqrt(mean_square + EPSILON) * gain[...]).astype(BF16)
    raw = total[:, lat:]
    turned = jnp.where(lane < rope // 2, -pltpu.roll(raw, LANES - rope // 2, 1), pltpu.roll(raw, rope // 2, 1))
    rotated = jnp.where(lane < rope, raw * cosine + turned * sine, penalty)
    kv[0, 0, own_rows, lat:] = rotated.astype(BF16)

    def x_copy(p, e):
        place = kv.at[0, p, own_rows]
        return remote(place, place, x_ssem.at[p, e], x_rsem.at[p, e], x_peer[e])

    def to_sibling(d):
        part_rows = pl.ds(pl.multiple_of(up(x, nx - d, nx) * sl, sl), sl)
        return remote(kv.at[0, 0, part_rows], kv.at[1, 0, part_rows], s0_ssem.at[d], s0_rsem.at[d], sibling)

    def y_copy(d, e):
        part_rows = pl.ds(pl.multiple_of(up(x, nx - e, nx) * sl, sl), sl)
        return remote(
            kv.at[0, 0, part_rows], kv.at[0, y_place[d], part_rows], y_ssem.at[d, e], y_rsem.at[d, e], y_peer[d]
        )

    for e in range(1, nx):
        x_copy(0, e).start()
    to_sibling(0).start()
    for d in y_order[1:]:
        y_copy(d, 0).start()
    z_receive(2)
    z_send(3)
    for e in range(1, nx):
        x_copy(0, e).wait_recv()
        to_sibling(e).start()
        for d in y_near:
            y_copy(d, e).start()

    ml[...] = jnp.zeros(ml.shape, F32)
    for copy in n1:
        copy.wait_recv()
    loads[10].wait()
    for d in y_far:
        y_copy(d, 0).wait_recv()
        for e in range(1, nx):
            x_copy(y_place[d], e).start()
    for e in range(nx):
        to_sibling(e).wait_recv()

    def chunk_keys(pieces):
        return jnp.concatenate([kv[i, j] for i, j in pieces], axis=0)

    def transpose_values(pieces, first=0):
        for k, (i, j) in enumerate(pieces):
            vt[:, (first + k) * half : (first + k + 1) * half] = kv[i, j, :, 0:lat].T

    per_head = ny * tr
    lane = lax.broadcasted_iota(jnp.int32, (per_head, LANES), 1)
    line = lax.broadcasted_iota(jnp.int32, (per_head, LANES), 0)

    def absorb(s):
        first_row = up(z, nz - s, nz) * (ny * rows)
        request = jnp.zeros((per_head, LANES), jnp.int32)
        for i in range(ny * rows):
            here = (line // tr == i // rows) & (line % rows == i % rows)
            request = jnp.where(here, rowreq[first_row + i], request)
        one_hot = jnp.where(lane - rope == request, 1.0, 0.0)
        for h in range(hs):
            here = pl.ds(h * per_head, per_head)
            qa[s, here, 0:lat] = nn(qg[s, h].reshape(per_head, LANES), ku[h]).astype(BF16)
            pair = qg[s, hs + h // 2].reshape(per_head, LANES).astype(F32)
            if h % 2:
                pair = pltpu.roll(pair, rope, 1)
            qa[s, here, lat:] = jnp.where(lane < rope, pair, one_hot).astype(BF16)

    def first_keys(keys, values, slots):
        scores = [nt(keys, qa[s]) for s in slots]
        tops = [jnp.max(score, axis=0, keepdims=True) for score in scores]
        weights = [jnp.exp2((score - top) * scale) for score, top in zip(scores, tops)]
        sums = [jnp.sum(weight, axis=0, keepdims=True) for weight in weights]
        mixed = [nn(values, weight.astype(BF16)) for weight in weights]
        return tops, sums, mixed

    def next_keys(scores, values, slots):
        before = [ml[s, 0:1, :] for s in slots]
        sums = [ml[s, 1:2, :] for s in slots]
        tops = [jnp.maximum(old, jnp.max(score, axis=0, keepdims=True)) for old, score in zip(before, scores)]
        weights = [jnp.exp2((score - top) * scale) for score, top in zip(scores, tops)]
        keeps = [jnp.exp2((old - top) * scale) for old, top in zip(before, tops)]
        sums = [
            old * keep + jnp.sum(weight, axis=0, keepdims=True) for old, keep, weight in zip(sums, keeps, weights)
        ]
        mixed = [
            ot[s] * keep + nn(values, weight.astype(BF16)) for s, keep, weight in zip(slots, keeps, weights)
        ]
        return tops, sums, mixed

    def put(slots, tops, sums, mixed):
        for s, top, total, mix in zip(slots, tops, sums, mixed):
            ml[s, 0:1, :] = top
            ml[s, 1:2, :] = total
            if mix is not None:
                ot[s] = mix

    at_once = min(AT_ONCE, nz)
    bunches = [z_order[i : i + at_once] for i in range(0, nz, at_once)]
    own_pieces = [(0, 0), (1, 0)]
    transpose_values(own_pieces)
    for slots in bunches:
        for s in slots:
            if nz > 1 and s == nz // 2:
                z_far.wait_recv()
            elif s:
                z_receive(min(s, nz - s))
            absorb(s)
        put(slots, *first_keys(chunk_keys(own_pieces), vt[:, 0 : CORES * half], slots))

    sides = [c, 1 - c]
    outs = []
    for i in range(CORES):
        rope_t[i] = kv[i, 0, :, lat:].astype(F32).T[0:rope].astype(BF16)
        place = pl.ds(pl.multiple_of(sides[i] * half, half), half)
        outs.append(pltpu.make_async_copy(kv.at[i, 0, :, pl.ds(0, lat)], lat_o.at[place], o_sem.at[2 * i]))
        outs.append(pltpu.make_async_copy(rope_t.at[i], rope_o.at[:, place], o_sem.at[2 * i + 1]))
    for copy in outs:
        copy.start()

    fresh = ny * tr
    new_keys = nkv[...].reshape(fresh, wide)
    key_of = lax.broadcasted_iota(jnp.int32, (fresh, group), 0)
    query_of = lax.broadcasted_iota(jnp.int32, (fresh, group), 1) % fresh
    allowed = (
        (key_of // tr == query_of // tr)
        & (key_of % rows == query_of % rows)
        & ((key_of % tr) // rows <= (query_of % tr) // rows)
    )
    scores = jnp.where(allowed, nt(new_keys, qa[0]), MASKED)
    put([0], *next_keys([scores], new_keys[:, 0:lat].astype(F32).T.astype(BF16), [0]))

    pieces = [(i, p) for i in range(CORES) for p in range(1, ny)]
    forwards = []
    for p in range(1, ny):
        d = y_order[p]
        for e in range(1, nx):
            if d in y_near:
                y_copy(d, e).wait_recv()
            else:
                x_copy(p, e).wait_recv()
        if d in y_near:
            y_copy(d, 0).wait_recv()
        forwards.append(remote(kv.at[0, p], kv.at[1, p], s_ssem.at[p], s_rsem.at[p], sibling))
        forwards[-1].start()
    transpose_values(pieces[: ny - 1])
    for copy in forwards:
        copy.wait_recv()
    transpose_values(pieces[ny - 1 :], ny - 1)

    def back(s):
        to = dev(up(z, nz - s, nz), y, x, c)
        return (
            remote(u_snd.at[s], u_rcv.at[s], u_ssem.at[s], u_rsem.at[s], to),
            remote(ml.at[s], ml_rcv.at[s], m_ssem.at[s], m_rsem.at[s], to),
        )

    of_head = lax.broadcasted_iota(jnp.int32, (LANES, group), 1) // (group // hs)
    own_values = None
    last_order = z_order[::-1]
    for i in range(0, nz, LAST_AT_ONCE):
        slots = last_order[i : i + LAST_AT_ONCE]
        keys = chunk_keys(pieces)
        tops, sums, mixed = next_keys([nt(keys, qa[s]) for s in slots], vt[:, 0 : len(pieces) * half], slots)
        put(slots, tops, sums, [None] * len(slots))
        for s, mix in zip(slots, mixed):
            every = nn(vut[...], mix.astype(BF16))
            values = every[0:LANES]
            for h in range(1, hs):
                values = jnp.where(of_head == h, every[h * LANES : (h + 1) * LANES], values)
            if s:
                u_snd[s] = values.astype(BF16)
            else:
                own_values = values
        for s in slots:
            if s:
                for copy in back(s):
                    copy.start()

    top = ml[0, 0:1, :]
    for s in range(1, nz):
        for copy in back(s):
            copy.wait_recv()
        top = jnp.maximum(top, ml_rcv[s, 0:1, :])
    keep = jnp.exp2((ml[0, 0:1, :] - top) * scale)
    numerator = own_values * keep
    denominator = ml[0, 1:2, :] * keep
    for s in range(1, nz):
        keep = jnp.exp2((ml_rcv[s, 0:1, :] - top) * scale)
        numerator = numerator + u_rcv[s].astype(F32) * keep
        denominator = denominator + ml_rcv[s, 1:2, :] * keep
    values = (numerator / denominator).T.astype(BF16)
    o_snd[...] = values.reshape(hs, ny, tr, LANES)
    own_heads = pl.ds(y * hs, hs)
    back_y = [
        remote(o_snd.at[:, up(y, d, ny)], o_rcv.at[own_heads], h_ssem.at[d], h_rsem.at[d], y_peer[d])
        for d in range(1, ny)
    ]
    for copy in back_y:
        copy.start()
    o_rcv[own_heads] = o_snd[:, y]
    for copy in back_y:
        copy.wait_recv()
    for h in range(heads):
        of[:, h, :] = o_rcv[h].astype(F32)
    hv[...] = of[...].astype(BF16)
    hv_copy = pltpu.make_async_copy(hv, hv_o, o_sem.at[2 * CORES])
    hv_copy.start()

    a_copy.wait_send()
    for copy in q1 + n1 + b + back_y:
        copy.wait_send()
    for copies in z_steps.values():
        for copy in copies:
            copy.wait_send()
    if z_far is not None:
        z_far.wait_send()
    for s in range(1, nz):
        for copy in back(s):
            copy.wait_send()
    for e in range(nx):
        if e:
            x_copy(0, e).wait_send()
            for d in y_far:
                x_copy(y_place[d], e).wait_send()
        to_sibling(e).wait_send()
        for d in y_near + (y_far if e == 0 else []):
            y_copy(d, e).wait_send()
    for copy in forwards:
        copy.wait_send()
    for copy in outs:
        copy.wait()
    hv_copy.wait()


def place_outputs(a, b, c, a_out, b_out, c_out, sem):
    copies = [pltpu.make_async_copy(i, o, sem.at[k]) for k, (i, o) in enumerate(((a, a_out), (b, b_out), (c, c_out)))]
    for copy in copies:
        copy.start()
    for copy in copies:
        copy.wait()


def local(
    prompt_hidden,
    latent_down,
    rope_down,
    latent_gain,
    request_lengths,
    row_request,
    query_nope,
    query_rope,
    new_latent,
    new_rope,
    key_up,
    value_up,
):
    ny = Y_SIZE
    nz = lax.axis_size("ctx") // ny
    nx = lax.axis_size("head") // CORES
    tok, depth = prompt_hidden.shape
    half = tok // CORES
    sl = half // nx
    steps, rows, heads, nope = query_nope.shape
    rope = query_rope.shape[-1]
    lat = key_up.shape[-1]
    tr = steps * rows
    hs = heads // ny
    group = hs * ny * tr
    wide = lat + LANES
    scale = math.log2(math.e) / math.sqrt(nope + rope)
    cfg = (nz, ny, nx, half, sl, lat, heads, hs, tr, rows, steps, group, rope, scale)
    spare = np.zeros((1, LANES), np.float32)
    frequency = 10000.0 ** (-2.0 * np.arange(rope // 2, dtype=np.float32) / rope)
    spare[0, :rope] = np.tile(frequency.astype(np.float32), 2)
    dma = pltpu.SemaphoreType.DMA
    vmem = pltpu.VMEM
    scratch = [
        vmem((2, half, depth), BF16),
        vmem((depth, lat), BF16),
        vmem((LANES, depth), BF16),
        vmem((1, lat), F32),
        vmem((tr, heads, nope), BF16),
        vmem((tr, heads, rope), BF16),
        vmem((steps, rows, lat), BF16),
        vmem((steps, rows, rope), BF16),
        vmem((hs, nope, lat), BF16),
        vmem((hs, lat, LANES), BF16),
        vmem((1, LANES), F32),
        dma((12,)),
        vmem((half, wide), BF16),
        vmem((half, wide), BF16),
        vmem((half, wide), F32),
        vmem((nx, sl, wide), BF16),
        vmem((nx, sl, wide), BF16),
        dma((2,)),
        dma((nx,)),
        dma((nx,)),
        vmem((CORES, ny, half, wide), BF16),
        vmem((lat, max(1, ny - 1) * tok), BF16),
        vmem((hs * LANES, lat), BF16),
        vmem((CORES, rope, half), BF16),
        dma((ny, nx)),
        dma((ny, nx)),
        dma((nx,)),
        dma((nx,)),
        dma((ny,)),
        dma((ny,)),
        dma((ny, nx)),
        dma((ny, nx)),
        dma((2 * CORES + 1,)),
        vmem((2, tr, heads, LANES), F32),
        vmem((ny, hs + hs // 2, tr, LANES), BF16),
        vmem((nz, hs + hs // 2, ny, tr, LANES), BF16),
        vmem((nz, group, wide), BF16),
        vmem((ny, tr, wide), BF16),
        dma((ny,)),
        dma((ny,)),
        dma((ny,)),
        dma((ny,)),
        dma((2, nz // 2 + 1)),
        dma((2, nz // 2 + 1)),
        vmem((nz, lat, group), F32),
        vmem((nz, 8, group), F32),
        vmem((nz, LANES, group), BF16),
        vmem((nz, LANES, group), BF16),
        vmem((nz, 8, group), F32),
        dma((nz,)),
        dma((nz,)),
        dma((nz,)),
        dma((nz,)),
        vmem((hs, ny, tr, LANES), BF16),
        vmem((heads, tr, LANES), BF16),
        vmem((tr, heads, LANES), F32),
        vmem((tr, heads, LANES), BF16),
        dma((ny,)),
        dma((ny,)),
    ]
    anywhere = pl.BlockSpec(memory_space=pl.ANY)
    scalars = pl.BlockSpec(memory_space=pltpu.SMEM)
    latent_cache, rope_cache, head_values = pl.pallas_call(
        functools.partial(kernel, cfg),
        out_shape=(
            jax.ShapeDtypeStruct((tok, lat), BF16),
            jax.ShapeDtypeStruct((rope, tok), BF16),
            jax.ShapeDtypeStruct((tr, heads, LANES), BF16),
        ),
        in_specs=[anywhere] * 4 + [scalars] * 2 + [anywhere] * 7,
        out_specs=(anywhere,) * 3,
        scratch_shapes=scratch,
        compiler_params=pltpu.CompilerParams(
            collective_id=0, has_side_effects=True, vmem_limit_bytes=60 * 1024 * 1024
        ),
    )(
        prompt_hidden,
        latent_down,
        rope_down,
        latent_gain.reshape(1, lat),
        request_lengths,
        row_request,
        query_nope.reshape(tr, heads, nope),
        query_rope.reshape(tr, heads, rope),
        new_latent,
        new_rope,
        key_up,
        value_up,
        jnp.asarray(spare),
    )
    latent_cache, rope_cache, head_values = pl.pallas_call(
        place_outputs,
        out_shape=tuple(jax.ShapeDtypeStruct(a.shape, a.dtype) for a in (latent_cache, rope_cache, head_values)),
        in_specs=[pl.BlockSpec(memory_space=pltpu.VMEM)] * 3,
        out_specs=(anywhere,) * 3,
        scratch_shapes=[dma((3,))],
    )(latent_cache, rope_cache, head_values)
    return (latent_cache, rope_cache, head_values.reshape(steps, rows, heads, LANES))


def solution(mesh):
    placed = (
        P("ctx", "head"),
        P("head", None),
        P(None, "head"),
        P(),
        P(),
        P(),
        P(None, "ctx", "head", None),
        P(None, "ctx", "head", None),
        P(None, "ctx", None),
        P(None, "ctx", None),
        P("head", None, None),
        P("head", None, None),
    )
    return jax.shard_map(
        local,
        mesh=mesh,
        in_specs=placed,
        out_specs=(P("ctx", None), P(None, "ctx"), P(None, "ctx", "head", None)),
        check_vma=False,
    )
```

```python
import functools
import math

import jax
import jax.numpy as jnp
import numpy as np
from jax import lax
from jax.experimental import pallas as pl
from jax.experimental.pallas import tpu as pltpu
from jax.sharding import PartitionSpec as P

MESH = pl.DeviceIdType.MESH
EPSILON = 1e-6
MASKED = -1e30
Y_SIZE = 4
CORES = 2
LANES = 128
CUTS = 2
LAST_AT_ONCE = 2
PART = 2
JOIN = 2
AT_ONCE = 4
F32 = jnp.float32
BF16 = jnp.bfloat16


def nt(a, b):
    return lax.dot_general(a, b, (((1,), (1,)), ((), ())), preferred_element_type=F32)


def nn(a, b):
    return jnp.dot(a, b, preferred_element_type=F32)


def kernel(
    cfg,
    hid_h, ld_h, rd_h, gain_h, lens, rowreq, qn_h, qr_h, nl_h, nr_h, ku_h, vu_h, freq_h,
    lat_o, rope_o, hv_o,
    hid, ld, rd, gain, qn, qr, nl, nr, ku, vu, freq, loc,
    a_snd, a_rcv, part, b_snd, b_rcv, a_sem, b_ssem, b_rsem,
    kv, vt, vut, rope_t, x_ssem, x_rsem, s0_ssem, s0_rsem, s_ssem, s_rsem, y_ssem, y_rsem, o_sem,
    qf, q_snd, qg, qa, nkv, q1_ssem, q1_rsem, n1_ssem, n1_rsem, q2_ssem, q2_rsem,
    ot, ml, u_snd, u_rcv, ml_rcv, u_ssem, u_rsem, m_ssem, m_rsem,
    o_snd, o_rcv, of, hv, h_ssem, h_rsem,
):
    nz, ny, nx, half, sl, lat, heads, hs, tr, rows, steps, group, rope, scale = cfg
    wide = lat + LANES
    ctx = lax.axis_index("ctx")
    head = lax.axis_index("head")
    z, y = ctx // ny, ctx % ny
    x, c = head // CORES, head % CORES

    def dev(zz, yy, xx, cc):
        return (zz * ny + yy, xx * CORES + cc)

    def up(value, by, size):
        return (value + by) % size

    def remote(src, dst, ssem, rsem, device):
        return pltpu.make_async_remote_copy(
            src_ref=src, dst_ref=dst, send_sem=ssem, recv_sem=rsem, device_id=device, device_id_type=MESH
        )

    sibling = dev(z, y, x, 1 - c)
    x_peer = [None] + [dev(z, y, up(x, d, nx), c) for d in range(1, nx)]
    y_peer = [None] + [dev(z, up(y, d, ny), x, c) for d in range(1, ny)]

    y_order = [0, 1] + ([ny - 1] + list(range(2, ny - 1)) if ny > 2 else [])
    y_place = {d: i for i, d in enumerate(y_order)}
    y_near = y_order[1:3]
    y_far = y_order[3:]

    loads = [
        (qn_h, qn),
        (qr_h, qr),
        (hid_h.at[pl.ds(pl.multiple_of((1 - c) * half, half), half)], hid.at[0]),
        (ld_h, ld),
        (rd_h, rd.at[pl.ds(0, rope)]),
        (hid_h.at[pl.ds(pl.multiple_of(c * half, half), half)], hid.at[1]),
        (nl_h, nl),
        (nr_h, nr),
        (gain_h, gain),
        (freq_h, freq),
        (ku_h.at[pl.ds(y * hs, hs)], ku),
        (vu_h.at[pl.ds(y * hs, hs)], vu),
    ]
    loads = [pltpu.make_async_copy(src, dst, loc.at[i]) for i, (src, dst) in enumerate(loads)]
    for load in loads:
        load.start()

    barrier = pltpu.get_barrier_semaphore()
    peers = [sibling] + x_peer[1:] + y_peer[1:] + [dev(up(z, d, nz), y, x, c) for d in range(1, nz)]
    for peer in peers:
        pl.semaphore_signal(barrier, inc=1, device_id=peer, device_id_type=MESH)

    loads[0].wait()
    loads[1].wait()
    qf[0] = qn[...].astype(F32)
    qf[1, :, :, 0:rope] = qr[...].astype(F32)
    lane = lax.broadcasted_iota(jnp.int32, (tr, LANES), 1)
    for h in range(heads):
        q_snd[h // hs, h % hs] = qf[0, :, h, :].astype(BF16)
    for h in range(0, heads, 2):
        pair = jnp.where(lane < rope, qf[1, :, h, :], pltpu.roll(qf[1, :, h + 1, :], rope, 1))
        q_snd[h // hs, hs + (h % hs) // 2] = pair.astype(BF16)
    qg[0, :, y] = q_snd[y]
    loads[6].wait()
    loads[7].wait()
    nkv[y, :, 0:lat] = nl[...].reshape(tr, lat)
    nkv[y, :, lat:] = jnp.zeros((tr, LANES), BF16)
    nkv[y, :, lat : lat + rope] = nr[...].reshape(tr, rope)

    rd[pl.ds(rope, LANES - rope)] = jnp.zeros((LANES - rope, rd.shape[1]), BF16)
    for i in (2, 3, 4):
        loads[i].wait()
    a_snd[:, 0:lat] = nn(hid[0], ld[...]).astype(BF16)
    a_snd[:, lat:] = nt(hid[0], rd[...]).astype(BF16)

    pl.semaphore_wait(barrier, len(peers))
    a_copy = remote(a_snd, a_rcv, a_sem.at[0], a_sem.at[1], sibling)
    a_copy.start()
    q1, n1 = [], []
    for d in range(1, ny):
        to = up(y, d, ny)
        q1.append(
            remote(q_snd.at[to], qg.at[0, :, y], q1_ssem.at[d], q1_rsem.at[d], y_peer[d])
        )
        n1.append(remote(nkv.at[y], nkv.at[y], n1_ssem.at[d], n1_rsem.at[d], y_peer[d]))
    for copy in q1 + n1:
        copy.start()

    loads[5].wait()
    part[:, 0:lat] = nn(hid[1], ld[...])
    part[:, lat:] = nt(hid[1], rd[...])

    for copy in q1:
        copy.wait_recv()

    def z_copies(step):
        forth = remote(
            qg.at[step - 1], qg.at[step], q2_ssem.at[0, step], q2_rsem.at[0, step], dev(up(z, 1, nz), y, x, c)
        )
        back_slot = (nz - step + 1) % nz
        back = remote(
            qg.at[back_slot],
            qg.at[nz - step],
            q2_ssem.at[1, step],
            q2_rsem.at[1, step],
            dev(up(z, nz - 1, nz), y, x, c),
        )
        return forth, back

    z_far = None
    if nz > 1:
        z_far = remote(
            qg.at[0],
            qg.at[nz // 2],
            q2_ssem.at[0, nz // 2],
            q2_rsem.at[0, nz // 2],
            dev(up(z, nz // 2, nz), y, x, c),
        )
    z_steps = {step: z_copies(step) for step in range(1, nz // 2)}
    z_received = set()

    def z_receive(step):
        if step in z_steps and step not in z_received:
            z_received.add(step)
            for copy in z_steps[step]:
                copy.wait_recv()

    def z_send(step):
        if step in z_steps:
            for copy in z_steps[step]:
                copy.start()

    z_order = [(i + 1) // 2 if i % 2 else (nz - i // 2) % nz for i in range(nz)]
    z_send(1)

    a_copy.wait_recv()
    part[...] += a_rcv[...].astype(F32)
    b_snd[...] = part[...].astype(BF16).reshape(nx, sl, wide)
    cut = sl // CUTS
    x_order = ([1, nx - 1] + list(range(2, nx - 1))) if nx > 2 else list(range(1, nx))
    b = {}
    for u in range(CUTS):
        for d in x_order:
            rows_u = pl.ds(u * cut, cut)
            b[d, u] = remote(
                b_snd.at[up(x, d, nx), rows_u], b_rcv.at[d, rows_u], b_ssem.at[d, u], b_rsem.at[d, u], x_peer[d]
            )
            b[d, u].start()
    z_receive(1)
    z_send(2)
    if z_far is not None:
        z_far.start()

    loads[11].wait()
    for h in range(hs):
        vut[pl.ds(h * LANES, LANES)] = vu[h].T
    loads[8].wait()
    loads[9].wait()
    position = (ctx * (half * CORES) + c * half + x * sl) + lax.broadcasted_iota(jnp.int32, (sl, LANES), 0)
    owner = jnp.zeros((sl, LANES), jnp.int32)
    start = jnp.zeros((sl, LANES), jnp.int32)
    end = jnp.int32(0)
    for r in range(lens.shape[0] - 1):
        end = end + lens[r]
        owner = owner + jnp.where(position >= end, 1, 0)
        start = jnp.where(position >= end, end, start)
    angle = freq[...] * (position - start).astype(F32)
    cosine, sine = jnp.cos(angle), jnp.sin(angle)
    lane = lax.broadcasted_iota(jnp.int32, (sl, LANES), 1)
    penalty = jnp.where((lane >= rope) & (lane < rope + lens.shape[0]) & (lane - rope != owner), MASKED, 0.0)

    def rows_of(e, u):
        return pl.ds(pl.multiple_of(up(x, nx - e, nx) * sl + u * cut, cut), cut)

    def x_copy(p, e, u):
        place = kv.at[0, p, rows_of(0, u)]
        return remote(place, place, x_ssem.at[p, e, u], x_rsem.at[p, e, u], x_peer[e])

    def to_sibling(e, u):
        there = rows_of(e, u)
        return remote(kv.at[0, 0, there], kv.at[1, 0, there], s0_ssem.at[e, u], s0_rsem.at[e, u], sibling)

    def y_copy(d, e, u):
        there = rows_of(e, u)
        return remote(
            kv.at[0, 0, there], kv.at[0, y_place[d], there], y_ssem.at[d, e, u], y_rsem.at[d, e, u], y_peer[d]
        )

    for u in range(CUTS):
        some = slice(u * cut, (u + 1) * cut)
        total = part[rows_of(0, u), :]
        for d in x_order:
            b[d, u].wait_recv()
            total = total + b_rcv[d, some].astype(F32)
        latent = total[:, 0:lat]
        mean_square = jnp.mean(latent * latent, axis=-1, keepdims=True)
        kv[0, 0, rows_of(0, u), 0:lat] = (latent * lax.rsqrt(mean_square + EPSILON) * gain[...]).astype(BF16)
        raw = total[:, lat:]
        low = lane[some] < rope // 2
        turned = jnp.where(low, -pltpu.roll(raw, LANES - rope // 2, 1), pltpu.roll(raw, rope // 2, 1))
        rotated = jnp.where(lane[some] < rope, raw * cosine[some] + turned * sine[some], penalty[some])
        kv[0, 0, rows_of(0, u), lat:] = rotated.astype(BF16)
        for e in x_order:
            x_copy(0, e, u).start()
        to_sibling(0, u).start()
        for d in y_order[1:]:
            y_copy(d, 0, u).start()
    z_receive(2)
    z_send(3)
    for u in range(CUTS):
        for e in x_order:
            x_copy(0, e, u).wait_recv()
            for d in y_near:
                y_copy(d, e, u).start()
            to_sibling(e, u).start()
        for d in y_far:
            y_copy(d, 0, u).wait_recv()
            for e in x_order:
                x_copy(y_place[d], e, u).start()

    ml[...] = jnp.zeros(ml.shape, F32)
    for copy in n1:
        copy.wait_recv()
    loads[10].wait()
    for u in range(CUTS):
        for e in range(nx):
            to_sibling(e, u).wait_recv()

    def chunk_keys(pieces):
        return jnp.concatenate([kv[i, j] for i, j in pieces], axis=0)

    def transpose_values(pieces, first=0):
        for k, (i, j) in enumerate(pieces):
            vt[:, (first + k) * half : (first + k + 1) * half] = kv[i, j, :, 0:lat].T

    per_head = ny * tr
    lane = lax.broadcasted_iota(jnp.int32, (per_head, LANES), 1)
    line = lax.broadcasted_iota(jnp.int32, (per_head, LANES), 0)

    def absorb(s):
        first_row = up(z, nz - s, nz) * (ny * rows)
        request = jnp.zeros((per_head, LANES), jnp.int32)
        for i in range(ny * rows):
            here = (line // tr == i // rows) & (line % rows == i % rows)
            request = jnp.where(here, rowreq[first_row + i], request)
        one_hot = jnp.where(lane - rope == request, 1.0, 0.0)
        for h in range(hs):
            here = pl.ds(h * per_head, per_head)
            qa[s, here, 0:lat] = nn(qg[s, h].reshape(per_head, LANES), ku[h]).astype(BF16)
            pair = qg[s, hs + h // 2].reshape(per_head, LANES).astype(F32)
            if h % 2:
                pair = pltpu.roll(pair, rope, 1)
            qa[s, here, lat:] = jnp.where(lane < rope, pair, one_hot).astype(BF16)

    def joined(slots):
        return [slots[i : i + JOIN] for i in range(0, len(slots), JOIN)]

    def beside(ref, slots, row=None):
        parts = [ref[s] if row is None else ref[s, row : row + 1, :] for s in slots]
        return parts[0] if len(parts) == 1 else jnp.concatenate(parts, axis=1)

    def scores_of(keys, slots):
        parts = [qa[s] for s in slots]
        return nt(keys, parts[0] if len(parts) == 1 else jnp.concatenate(parts, axis=0))

    def first_keys(keys, values, bunch):
        scores = [scores_of(keys, slots) for slots in bunch]
        tops = [jnp.max(score, axis=0, keepdims=True) for score in scores]
        weights = [jnp.exp2((score - top) * scale) for score, top in zip(scores, tops)]
        sums = [jnp.sum(weight, axis=0, keepdims=True) for weight in weights]
        mixed = [nn(values, weight.astype(BF16)) for weight in weights]
        return tops, sums, mixed

    def next_keys(scores, values, bunch):
        before = [beside(ml, slots, 0) for slots in bunch]
        sums = [beside(ml, slots, 1) for slots in bunch]
        tops = [jnp.maximum(old, jnp.max(score, axis=0, keepdims=True)) for old, score in zip(before, scores)]
        weights = [jnp.exp2((score - top) * scale) for score, top in zip(scores, tops)]
        keeps = [jnp.exp2((old - top) * scale) for old, top in zip(before, tops)]
        sums = [
            old * keep + jnp.sum(weight, axis=0, keepdims=True) for old, keep, weight in zip(sums, keeps, weights)
        ]
        mixed = [
            beside(ot, slots) * keep + nn(values, weight.astype(BF16))
            for slots, keep, weight in zip(bunch, keeps, weights)
        ]
        return tops, sums, mixed

    def put(bunch, tops, sums, mixed):
        for slots, top, total, mix in zip(bunch, tops, sums, mixed):
            for k, s in enumerate(slots):
                here = slice(k * group, (k + 1) * group)
                ml[s, 0:1, :] = top[:, here]
                ml[s, 1:2, :] = total[:, here]
                if mix is not None:
                    ot[s] = mix[:, here]

    at_once = min(AT_ONCE, nz)
    bunches = [z_order[i : i + at_once] for i in range(0, nz, at_once)]
    own_pieces = [(0, 0), (1, 0)]
    transpose_values(own_pieces)
    for slots in bunches:
        for s in slots:
            if nz > 1 and s == nz // 2:
                z_far.wait_recv()
            elif s:
                z_receive(min(s, nz - s))
            absorb(s)
        bunch = joined(slots)
        put(bunch, *first_keys(chunk_keys(own_pieces), vt[:, 0 : CORES * half], bunch))

    sides = [c, 1 - c]
    outs = []
    for i in range(CORES):
        rope_t[i] = kv[i, 0, :, lat:].astype(F32).T[0:rope].astype(BF16)
        place = pl.ds(pl.multiple_of(sides[i] * half, half), half)
        outs.append(pltpu.make_async_copy(kv.at[i, 0, :, pl.ds(0, lat)], lat_o.at[place], o_sem.at[2 * i]))
        outs.append(pltpu.make_async_copy(rope_t.at[i], rope_o.at[:, place], o_sem.at[2 * i + 1]))
    for copy in outs:
        copy.start()

    fresh = ny * tr
    new_keys = nkv[...].reshape(fresh, wide)
    key_of = lax.broadcasted_iota(jnp.int32, (fresh, group), 0)
    query_of = lax.broadcasted_iota(jnp.int32, (fresh, group), 1) % fresh
    allowed = (
        (key_of // tr == query_of // tr)
        & (key_of % rows == query_of % rows)
        & ((key_of % tr) // rows <= (query_of % tr) // rows)
    )
    scores = jnp.where(allowed, nt(new_keys, qa[0]), MASKED)
    put([[0]], *next_keys([scores], new_keys[:, 0:lat].astype(F32).T.astype(BF16), [[0]]))

    pieces = [(i, p) for i in range(CORES) for p in range(1, ny)]
    forwards = []
    for p in range(1, ny):
        d = y_order[p]
        for u in range(CUTS):
            for e in range(1, nx):
                if d in y_near:
                    y_copy(d, e, u).wait_recv()
                else:
                    x_copy(p, e, u).wait_recv()
            if d in y_near:
                y_copy(d, 0, u).wait_recv()
        forwards.append(remote(kv.at[0, p], kv.at[1, p], s_ssem.at[p], s_rsem.at[p], sibling))
        forwards[-1].start()
    transpose_values(pieces[: ny - 1])
    for copy in forwards:
        copy.wait_recv()
    transpose_values(pieces[ny - 1 :], ny - 1)

    def back(s):
        to = dev(up(z, nz - s, nz), y, x, c)
        return (
            remote(u_snd.at[s], u_rcv.at[s], u_ssem.at[s], u_rsem.at[s], to),
            remote(ml.at[s, pl.ds(0, 2)], ml_rcv.at[s, pl.ds(0, 2)], m_ssem.at[s], m_rsem.at[s], to),
        )

    of_head = lax.broadcasted_iota(jnp.int32, (LANES, group), 1) // (group // hs)
    own_values = None
    last_order = z_order[::-1]
    if nz == 8:
        last_order = [3, 5, 4, 6, 2, 7, 1, 0]
    turns = [last_order[i : i + LAST_AT_ONCE] for i in range(0, nz, LAST_AT_ONCE)]
    key_parts = [chunk_keys(pieces[k : k + PART]) for k in range(0, len(pieces), PART)]
    scores = [scores_of(keys, turns[0]) for keys in key_parts]
    for turn, slots in enumerate(turns):
        before = beside(ml, slots, 0)
        top = before
        for score in scores:
            top = jnp.maximum(top, jnp.max(score, axis=0, keepdims=True))
        keep = jnp.exp2((before - top) * scale)
        total = beside(ml, slots, 1) * keep
        mix = beside(ot, slots) * keep
        weights, following = [], []
        for k, score in enumerate(scores):
            if turn + 1 < len(turns):
                following.append(scores_of(key_parts[k], turns[turn + 1]))
            weight = jnp.exp2((score - top) * scale)
            total = total + jnp.sum(weight, axis=0, keepdims=True)
            weights.append(weight.astype(BF16))
        weights = weights[0] if len(weights) == 1 else jnp.concatenate(weights, axis=0)
        mix = mix + nn(vt[:, 0 : len(pieces) * half], weights)
        scores = following
        put([slots], [top], [total], [None])
        for some, mix in [(slots, mix)]:
            every = nn(vut[...], mix.astype(BF16))
            for k, s in enumerate(some):
                mine = every[:, k * group : (k + 1) * group]
                values = mine[0:LANES]
                for h in range(1, hs):
                    values = jnp.where(of_head == h, mine[h * LANES : (h + 1) * LANES], values)
                if s:
                    u_snd[s] = values.astype(BF16)
                else:
                    own_values = values
        for s in slots:
            if s:
                for copy in back(s):
                    copy.start()

    top = ml[0, 0:1, :]
    for s in range(1, nz):
        for copy in back(s):
            copy.wait_recv()
        top = jnp.maximum(top, ml_rcv[s, 0:1, :])
    keep = jnp.exp2((ml[0, 0:1, :] - top) * scale)
    numerator = own_values * keep
    denominator = ml[0, 1:2, :] * keep
    for s in range(1, nz):
        keep = jnp.exp2((ml_rcv[s, 0:1, :] - top) * scale)
        numerator = numerator + u_rcv[s].astype(F32) * keep
        denominator = denominator + ml_rcv[s, 1:2, :] * keep
    values = (numerator / denominator).T.astype(BF16)
    o_snd[...] = values.reshape(hs, ny, tr, LANES)
    own_heads = pl.ds(y * hs, hs)
    back_y = [
        remote(o_snd.at[:, up(y, d, ny)], o_rcv.at[own_heads], h_ssem.at[d], h_rsem.at[d], y_peer[d])
        for d in range(1, ny)
    ]
    for copy in back_y:
        copy.start()
    o_rcv[own_heads] = o_snd[:, y]
    for copy in back_y:
        copy.wait_recv()
    for h in range(heads):
        of[:, h, :] = o_rcv[h].astype(F32)
    hv[...] = of[...].astype(BF16)
    hv_copy = pltpu.make_async_copy(hv, hv_o, o_sem.at[2 * CORES])
    hv_copy.start()

    a_copy.wait_send()
    for copy in q1 + n1 + list(b.values()) + back_y:
        copy.wait_send()
    for copies in z_steps.values():
        for copy in copies:
            copy.wait_send()
    if z_far is not None:
        z_far.wait_send()
    for s in range(1, nz):
        for copy in back(s):
            copy.wait_send()
    for e, u in [(e, u) for e in range(nx) for u in range(CUTS)]:
        if e:
            x_copy(0, e, u).wait_send()
            for d in y_far:
                x_copy(y_place[d], e, u).wait_send()
        to_sibling(e, u).wait_send()
        for d in y_near + (y_far if e == 0 else []):
            y_copy(d, e, u).wait_send()
    for copy in forwards:
        copy.wait_send()
    for copy in outs:
        copy.wait()
    hv_copy.wait()


def place_outputs(a, b, c, a_out, b_out, c_out, sem):
    copies = [pltpu.make_async_copy(i, o, sem.at[k]) for k, (i, o) in enumerate(((a, a_out), (b, b_out), (c, c_out)))]
    for copy in copies:
        copy.start()
    for copy in copies:
        copy.wait()


def local(
    prompt_hidden,
    latent_down,
    rope_down,
    latent_gain,
    request_lengths,
    row_request,
    query_nope,
    query_rope,
    new_latent,
    new_rope,
    key_up,
    value_up,
):
    ny = Y_SIZE
    nz = lax.axis_size("ctx") // ny
    nx = lax.axis_size("head") // CORES
    tok, depth = prompt_hidden.shape
    half = tok // CORES
    sl = half // nx
    steps, rows, heads, nope = query_nope.shape
    rope = query_rope.shape[-1]
    lat = key_up.shape[-1]
    tr = steps * rows
    hs = heads // ny
    group = hs * ny * tr
    wide = lat + LANES
    scale = math.log2(math.e) / math.sqrt(nope + rope)
    cfg = (nz, ny, nx, half, sl, lat, heads, hs, tr, rows, steps, group, rope, scale)
    spare = np.zeros((1, LANES), np.float32)
    frequency = 10000.0 ** (-2.0 * np.arange(rope // 2, dtype=np.float32) / rope)
    spare[0, :rope] = np.tile(frequency.astype(np.float32), 2)
    dma = pltpu.SemaphoreType.DMA
    vmem = pltpu.VMEM
    scratch = [
        vmem((2, half, depth), BF16),
        vmem((depth, lat), BF16),
        vmem((LANES, depth), BF16),
        vmem((1, lat), F32),
        vmem((tr, heads, nope), BF16),
        vmem((tr, heads, rope), BF16),
        vmem((steps, rows, lat), BF16),
        vmem((steps, rows, rope), BF16),
        vmem((hs, nope, lat), BF16),
        vmem((hs, lat, LANES), BF16),
        vmem((1, LANES), F32),
        dma((12,)),
        vmem((half, wide), BF16),
        vmem((half, wide), BF16),
        vmem((half, wide), F32),
        vmem((nx, sl, wide), BF16),
        vmem((nx, sl, wide), BF16),
        dma((2,)),
        dma((nx, CUTS)),
        dma((nx, CUTS)),
        vmem((CORES, ny, half, wide), BF16),
        vmem((lat, max(1, ny - 1) * tok), BF16),
        vmem((hs * LANES, lat), BF16),
        vmem((CORES, rope, half), BF16),
        dma((ny, nx, CUTS)),
        dma((ny, nx, CUTS)),
        dma((nx, CUTS)),
        dma((nx, CUTS)),
        dma((ny,)),
        dma((ny,)),
        dma((ny, nx, CUTS)),
        dma((ny, nx, CUTS)),
        dma((2 * CORES + 1,)),
        vmem((2, tr, heads, LANES), F32),
        vmem((ny, hs + hs // 2, tr, LANES), BF16),
        vmem((nz, hs + hs // 2, ny, tr, LANES), BF16),
        vmem((nz, group, wide), BF16),
        vmem((ny, tr, wide), BF16),
        dma((ny,)),
        dma((ny,)),
        dma((ny,)),
        dma((ny,)),
        dma((2, nz // 2 + 1)),
        dma((2, nz // 2 + 1)),
        vmem((nz, lat, group), F32),
        vmem((nz, 8, group), F32),
        vmem((nz, LANES, group), BF16),
        vmem((nz, LANES, group), BF16),
        vmem((nz, 8, group), F32),
        dma((nz,)),
        dma((nz,)),
        dma((nz,)),
        dma((nz,)),
        vmem((hs, ny, tr, LANES), BF16),
        vmem((heads, tr, LANES), BF16),
        vmem((tr, heads, LANES), F32),
        vmem((tr, heads, LANES), BF16),
        dma((ny,)),
        dma((ny,)),
    ]
    anywhere = pl.BlockSpec(memory_space=pl.ANY)
    scalars = pl.BlockSpec(memory_space=pltpu.SMEM)
    latent_cache, rope_cache, head_values = pl.pallas_call(
        functools.partial(kernel, cfg),
        out_shape=(
            jax.ShapeDtypeStruct((tok, lat), BF16),
            jax.ShapeDtypeStruct((rope, tok), BF16),
            jax.ShapeDtypeStruct((tr, heads, LANES), BF16),
        ),
        in_specs=[anywhere] * 4 + [scalars] * 2 + [anywhere] * 7,
        out_specs=(anywhere,) * 3,
        scratch_shapes=scratch,
        compiler_params=pltpu.CompilerParams(
            collective_id=0, has_side_effects=True, vmem_limit_bytes=60 * 1024 * 1024
        ),
    )(
        prompt_hidden,
        latent_down,
        rope_down,
        latent_gain.reshape(1, lat),
        request_lengths,
        row_request,
        query_nope.reshape(tr, heads, nope),
        query_rope.reshape(tr, heads, rope),
        new_latent,
        new_rope,
        key_up,
        value_up,
        jnp.asarray(spare),
    )
    latent_cache, rope_cache, head_values = pl.pallas_call(
        place_outputs,
        out_shape=tuple(jax.ShapeDtypeStruct(a.shape, a.dtype) for a in (latent_cache, rope_cache, head_values)),
        in_specs=[pl.BlockSpec(memory_space=pltpu.VMEM)] * 3,
        out_specs=(anywhere,) * 3,
        scratch_shapes=[dma((3,))],
    )(latent_cache, rope_cache, head_values)
    return (latent_cache, rope_cache, head_values.reshape(steps, rows, heads, LANES))


def solution(mesh):
    placed = (
        P("ctx", "head"),
        P("head", None),
        P(None, "head"),
        P(),
        P(),
        P(),
        P(None, "ctx", "head", None),
        P(None, "ctx", "head", None),
        P(None, "ctx", None),
        P(None, "ctx", None),
        P("head", None, None),
        P("head", None, None),
    )
    return jax.shard_map(
        local,
        mesh=mesh,
        in_specs=placed,
        out_specs=(P("ctx", None), P(None, "ctx"), P(None, "ctx", "head", None)),
        check_vma=False,
    )
```

```python
import functools
import math

import jax
import jax.numpy as jnp
import numpy as np
from jax import lax
from jax.experimental import pallas as pl
from jax.experimental.pallas import tpu as pltpu
from jax.sharding import PartitionSpec as P

MESH = pl.DeviceIdType.MESH
EPSILON = 1e-6
MASKED = -1e30
Y_SIZE = 4
CORES = 2
LANES = 128
CUTS = 2
LAST_AT_ONCE = 2
PART = 2
JOIN = 2
AT_ONCE = 4
F32 = jnp.float32
BF16 = jnp.bfloat16


def nt(a, b):
    return lax.dot_general(a, b, (((1,), (1,)), ((), ())), preferred_element_type=F32)


def nn(a, b):
    return jnp.dot(a, b, preferred_element_type=F32)


def kernel(
    cfg,
    hid_h, ld_h, rd_h, gain_h, lens, rowreq, qn_h, qr_h, nl_h, nr_h, ku_h, vu_h, freq_h,
    lat_o, rope_o, hv_o,
    hid, ld, rd, gain, qn, qr, nl, nr, ku, vu, freq, loc,
    a_snd, a_rcv, part, b_snd, b_rcv, a_sem, b_ssem, b_rsem,
    kv, vt, vut, rope_t, x_ssem, x_rsem, s0_ssem, s0_rsem, s_ssem, s_rsem, y_ssem, y_rsem, o_sem,
    qf, q_snd, qg, qa, nkv, q1_ssem, q1_rsem, n1_ssem, n1_rsem, q2_ssem, q2_rsem,
    ot, ml, u_snd, u_rcv, ml_rcv, u_ssem, u_rsem, m_ssem, m_rsem,
    o_snd, o_rcv, of, hv, h_ssem, h_rsem,
):
    nz, ny, nx, half, sl, lat, heads, hs, tr, rows, steps, group, rope, scale = cfg
    wide = lat + LANES
    ctx = lax.axis_index("ctx")
    head = lax.axis_index("head")
    z, y = ctx // ny, ctx % ny
    x, c = head // CORES, head % CORES

    def dev(zz, yy, xx, cc):
        return (zz * ny + yy, xx * CORES + cc)

    def up(value, by, size):
        return (value + by) % size

    def remote(src, dst, ssem, rsem, device):
        return pltpu.make_async_remote_copy(
            src_ref=src, dst_ref=dst, send_sem=ssem, recv_sem=rsem, device_id=device, device_id_type=MESH
        )

    sibling = dev(z, y, x, 1 - c)
    x_peer = [None] + [dev(z, y, up(x, d, nx), c) for d in range(1, nx)]
    y_peer = [None] + [dev(z, up(y, d, ny), x, c) for d in range(1, ny)]

    y_order = [0, 1] + ([ny - 1] + list(range(2, ny - 1)) if ny > 2 else [])
    y_place = {d: i for i, d in enumerate(y_order)}
    y_near = y_order[1:3]
    y_far = y_order[3:]

    loads = [
        (qn_h, qn),
        (qr_h, qr),
        (hid_h.at[pl.ds(pl.multiple_of((1 - c) * half, half), half)], hid.at[0]),
        (ld_h, ld),
        (rd_h, rd.at[pl.ds(0, rope)]),
        (hid_h.at[pl.ds(pl.multiple_of(c * half, half), half)], hid.at[1]),
        (nl_h, nl),
        (nr_h, nr),
        (gain_h, gain),
        (freq_h, freq),
        (ku_h.at[pl.ds(y * hs, hs)], ku),
        (vu_h.at[pl.ds(y * hs, hs)], vu),
    ]
    loads = [pltpu.make_async_copy(src, dst, loc.at[i]) for i, (src, dst) in enumerate(loads)]
    for load in loads:
        load.start()

    barrier = pltpu.get_barrier_semaphore()
    peers = [sibling] + x_peer[1:] + y_peer[1:] + [dev(up(z, d, nz), y, x, c) for d in range(1, nz)]
    for peer in peers:
        pl.semaphore_signal(barrier, inc=1, device_id=peer, device_id_type=MESH)

    loads[0].wait()
    loads[1].wait()
    qf[0] = qn[...].astype(F32)
    qf[1, :, :, 0:rope] = qr[...].astype(F32)
    lane = lax.broadcasted_iota(jnp.int32, (tr, LANES), 1)
    for h in range(heads):
        q_snd[h // hs, h % hs] = qf[0, :, h, :].astype(BF16)
    for h in range(0, heads, 2):
        pair = jnp.where(lane < rope, qf[1, :, h, :], pltpu.roll(qf[1, :, h + 1, :], rope, 1))
        q_snd[h // hs, hs + (h % hs) // 2] = pair.astype(BF16)
    qg[0, y] = q_snd[y]
    loads[6].wait()
    loads[7].wait()
    nkv[y, :, 0:lat] = nl[...].reshape(tr, lat)
    nkv[y, :, lat:] = jnp.zeros((tr, LANES), BF16)
    nkv[y, :, lat : lat + rope] = nr[...].reshape(tr, rope)

    rd[pl.ds(rope, LANES - rope)] = jnp.zeros((LANES - rope, rd.shape[1]), BF16)
    for i in (2, 3, 4):
        loads[i].wait()
    a_snd[:, 0:lat] = nn(hid[0], ld[...]).astype(BF16)
    a_snd[:, lat:] = nt(hid[0], rd[...]).astype(BF16)

    pl.semaphore_wait(barrier, len(peers))
    a_copy = remote(a_snd, a_rcv, a_sem.at[0], a_sem.at[1], sibling)
    a_copy.start()
    q1, n1 = [], []
    for d in range(1, ny):
        to = up(y, d, ny)
        q1.append(
            remote(q_snd.at[to], qg.at[0, y], q1_ssem.at[d], q1_rsem.at[d], y_peer[d])
        )
        n1.append(remote(nkv.at[y], nkv.at[y], n1_ssem.at[d], n1_rsem.at[d], y_peer[d]))
    z_order = [(i + 1) // 2 if i % 2 else (nz - i // 2) % nz for i in range(nz)]

    def z_copy(d, k):
        source = up(y, ny - d, ny)
        return remote(
            qg.at[0, source],
            qg.at[k, source],
            q2_ssem.at[d, k],
            q2_rsem.at[d, k],
            dev(up(z, k, nz), y, x, c),
        )

    for copy in q1:
        copy.start()
    for k in z_order[1:]:
        z_copy(0, k).start()

    loads[5].wait()
    part[:, 0:lat] = nn(hid[1], ld[...])
    part[:, lat:] = nt(hid[1], rd[...])

    a_copy.wait_recv()
    part[...] += a_rcv[...].astype(F32)
    b_snd[...] = part[...].astype(BF16).reshape(nx, sl, wide)
    cut = sl // CUTS
    x_order = ([1, nx - 1] + list(range(2, nx - 1))) if nx > 2 else list(range(1, nx))
    b = {}
    for u in range(CUTS):
        for d in x_order:
            rows_u = pl.ds(u * cut, cut)
            b[d, u] = remote(
                b_snd.at[up(x, d, nx), rows_u], b_rcv.at[d, rows_u], b_ssem.at[d, u], b_rsem.at[d, u], x_peer[d]
            )
            b[d, u].start()
    for copy in n1:
        copy.start()
    for d in range(1, ny):
        q1[d - 1].wait_recv()
        for k in z_order[1:]:
            z_copy(d, k).start()

    loads[11].wait()
    for h in range(hs):
        vut[pl.ds(h * LANES, LANES)] = vu[h].T
    loads[8].wait()
    loads[9].wait()
    position = (ctx * (half * CORES) + c * half + x * sl) + lax.broadcasted_iota(jnp.int32, (sl, LANES), 0)
    owner = jnp.zeros((sl, LANES), jnp.int32)
    start = jnp.zeros((sl, LANES), jnp.int32)
    end = jnp.int32(0)
    for r in range(lens.shape[0] - 1):
        end = end + lens[r]
        owner = owner + jnp.where(position >= end, 1, 0)
        start = jnp.where(position >= end, end, start)
    angle = freq[...] * (position - start).astype(F32)
    cosine, sine = jnp.cos(angle), jnp.sin(angle)
    lane = lax.broadcasted_iota(jnp.int32, (sl, LANES), 1)
    penalty = jnp.where((lane >= rope) & (lane < rope + lens.shape[0]) & (lane - rope != owner), MASKED, 0.0)

    def rows_of(e, u):
        return pl.ds(pl.multiple_of(up(x, nx - e, nx) * sl + u * cut, cut), cut)

    def x_copy(p, e, u):
        place = kv.at[0, p, rows_of(0, u)]
        return remote(place, place, x_ssem.at[p, e, u], x_rsem.at[p, e, u], x_peer[e])

    def to_sibling(e, u):
        there = rows_of(e, u)
        return remote(kv.at[0, 0, there], kv.at[1, 0, there], s0_ssem.at[e, u], s0_rsem.at[e, u], sibling)

    def y_copy(d, e, u):
        there = rows_of(e, u)
        return remote(
            kv.at[0, 0, there], kv.at[0, y_place[d], there], y_ssem.at[d, e, u], y_rsem.at[d, e, u], y_peer[d]
        )

    for u in range(CUTS):
        some = slice(u * cut, (u + 1) * cut)
        total = part[rows_of(0, u), :]
        for d in x_order:
            b[d, u].wait_recv()
            total = total + b_rcv[d, some].astype(F32)
        latent = total[:, 0:lat]
        mean_square = jnp.mean(latent * latent, axis=-1, keepdims=True)
        kv[0, 0, rows_of(0, u), 0:lat] = (latent * lax.rsqrt(mean_square + EPSILON) * gain[...]).astype(BF16)
        raw = total[:, lat:]
        low = lane[some] < rope // 2
        turned = jnp.where(low, -pltpu.roll(raw, LANES - rope // 2, 1), pltpu.roll(raw, rope // 2, 1))
        rotated = jnp.where(lane[some] < rope, raw * cosine[some] + turned * sine[some], penalty[some])
        kv[0, 0, rows_of(0, u), lat:] = rotated.astype(BF16)
        for e in x_order:
            x_copy(0, e, u).start()
        to_sibling(0, u).start()
        for d in y_order[1:]:
            y_copy(d, 0, u).start()
    for u in range(CUTS):
        for e in x_order:
            x_copy(0, e, u).wait_recv()
            for d in y_near:
                y_copy(d, e, u).start()
            to_sibling(e, u).start()
        for d in y_far:
            y_copy(d, 0, u).wait_recv()
            for e in x_order:
                x_copy(y_place[d], e, u).start()

    ml[...] = jnp.zeros(ml.shape, F32)
    for copy in n1:
        copy.wait_recv()
    loads[10].wait()
    for u in range(CUTS):
        for e in range(nx):
            to_sibling(e, u).wait_recv()

    def chunk_keys(pieces):
        return jnp.concatenate([kv[i, j] for i, j in pieces], axis=0)

    def transpose_values(pieces, first=0):
        for k, (i, j) in enumerate(pieces):
            vt[:, (first + k) * half : (first + k + 1) * half] = kv[i, j, :, 0:lat].T

    per_head = ny * tr
    lane = lax.broadcasted_iota(jnp.int32, (per_head, LANES), 1)
    line = lax.broadcasted_iota(jnp.int32, (per_head, LANES), 0)

    def absorb(s):
        first_row = up(z, nz - s, nz) * (ny * rows)
        request = jnp.zeros((per_head, LANES), jnp.int32)
        for i in range(ny * rows):
            here = (line // tr == i // rows) & (line % rows == i % rows)
            request = jnp.where(here, rowreq[first_row + i], request)
        one_hot = jnp.where(lane - rope == request, 1.0, 0.0)
        for h in range(hs):
            here = pl.ds(h * per_head, per_head)
            qa[s, here, 0:lat] = nn(qg[s, :, h].reshape(per_head, LANES), ku[h]).astype(BF16)
            pair = qg[s, :, hs + h // 2].reshape(per_head, LANES).astype(F32)
            if h % 2:
                pair = pltpu.roll(pair, rope, 1)
            qa[s, here, lat:] = jnp.where(lane < rope, pair, one_hot).astype(BF16)

    def joined(slots):
        return [slots[i : i + JOIN] for i in range(0, len(slots), JOIN)]

    def beside(ref, slots, row=None):
        parts = [ref[s] if row is None else ref[s, row : row + 1, :] for s in slots]
        return parts[0] if len(parts) == 1 else jnp.concatenate(parts, axis=1)

    def scores_of(keys, slots):
        parts = [qa[s] for s in slots]
        return nt(keys, parts[0] if len(parts) == 1 else jnp.concatenate(parts, axis=0))

    def first_keys(keys, values, bunch):
        scores = [scores_of(keys, slots) for slots in bunch]
        tops = [jnp.max(score, axis=0, keepdims=True) for score in scores]
        weights = [jnp.exp2((score - top) * scale) for score, top in zip(scores, tops)]
        sums = [jnp.sum(weight, axis=0, keepdims=True) for weight in weights]
        mixed = [nn(values, weight.astype(BF16)) for weight in weights]
        return tops, sums, mixed

    def next_keys(scores, values, bunch):
        before = [beside(ml, slots, 0) for slots in bunch]
        sums = [beside(ml, slots, 1) for slots in bunch]
        tops = [jnp.maximum(old, jnp.max(score, axis=0, keepdims=True)) for old, score in zip(before, scores)]
        weights = [jnp.exp2((score - top) * scale) for score, top in zip(scores, tops)]
        keeps = [jnp.exp2((old - top) * scale) for old, top in zip(before, tops)]
        sums = [
            old * keep + jnp.sum(weight, axis=0, keepdims=True) for old, keep, weight in zip(sums, keeps, weights)
        ]
        mixed = [
            beside(ot, slots) * keep + nn(values, weight.astype(BF16))
            for slots, keep, weight in zip(bunch, keeps, weights)
        ]
        return tops, sums, mixed

    def put(bunch, tops, sums, mixed):
        for slots, top, total, mix in zip(bunch, tops, sums, mixed):
            for k, s in enumerate(slots):
                here = slice(k * group, (k + 1) * group)
                ml[s, 0:1, :] = top[:, here]
                ml[s, 1:2, :] = total[:, here]
                if mix is not None:
                    ot[s] = mix[:, here]

    at_once = min(AT_ONCE, nz)
    bunches = [z_order[i : i + at_once] for i in range(0, nz, at_once)]
    own_pieces = [(0, 0), (1, 0)]
    transpose_values(own_pieces)
    for slots in bunches:
        for s in slots:
            if s:
                for d in range(ny):
                    z_copy(d, s).wait_recv()
            absorb(s)
        bunch = joined(slots)
        put(bunch, *first_keys(chunk_keys(own_pieces), vt[:, 0 : CORES * half], bunch))

    sides = [c, 1 - c]
    outs = []
    for i in range(CORES):
        rope_t[i] = kv[i, 0, :, lat:].astype(F32).T[0:rope].astype(BF16)
        place = pl.ds(pl.multiple_of(sides[i] * half, half), half)
        outs.append(pltpu.make_async_copy(kv.at[i, 0, :, pl.ds(0, lat)], lat_o.at[place], o_sem.at[2 * i]))
        outs.append(pltpu.make_async_copy(rope_t.at[i], rope_o.at[:, place], o_sem.at[2 * i + 1]))
    for copy in outs:
        copy.start()

    fresh = ny * tr
    new_keys = nkv[...].reshape(fresh, wide)
    key_of = lax.broadcasted_iota(jnp.int32, (fresh, group), 0)
    query_of = lax.broadcasted_iota(jnp.int32, (fresh, group), 1) % fresh
    allowed = (
        (key_of // tr == query_of // tr)
        & (key_of % rows == query_of % rows)
        & ((key_of % tr) // rows <= (query_of % tr) // rows)
    )
    scores = jnp.where(allowed, nt(new_keys, qa[0]), MASKED)
    put([[0]], *next_keys([scores], new_keys[:, 0:lat].astype(F32).T.astype(BF16), [[0]]))

    pieces = [(i, p) for i in range(CORES) for p in range(1, ny)]
    forwards = []
    for p in range(1, ny):
        d = y_order[p]
        for u in range(CUTS):
            for e in range(1, nx):
                if d in y_near:
                    y_copy(d, e, u).wait_recv()
                else:
                    x_copy(p, e, u).wait_recv()
            if d in y_near:
                y_copy(d, 0, u).wait_recv()
        forwards.append(remote(kv.at[0, p], kv.at[1, p], s_ssem.at[p], s_rsem.at[p], sibling))
        forwards[-1].start()
    transpose_values(pieces[: ny - 1])
    for copy in forwards:
        copy.wait_recv()
    transpose_values(pieces[ny - 1 :], ny - 1)

    def back(s):
        to = dev(up(z, nz - s, nz), y, x, c)
        return (
            remote(u_snd.at[s], u_rcv.at[s], u_ssem.at[s], u_rsem.at[s], to),
            remote(ml.at[s, pl.ds(0, 2)], ml_rcv.at[s, pl.ds(0, 2)], m_ssem.at[s], m_rsem.at[s], to),
        )

    of_head = lax.broadcasted_iota(jnp.int32, (LANES, group), 1) // (group // hs)
    own_values = None
    last_order = z_order[::-1]
    if nz == 8:
        last_order = [3, 5, 4, 6, 2, 7, 1, 0]
    turns = [last_order[i : i + LAST_AT_ONCE] for i in range(0, nz, LAST_AT_ONCE)]
    key_parts = [chunk_keys(pieces[k : k + PART]) for k in range(0, len(pieces), PART)]
    scores = [scores_of(keys, turns[0]) for keys in key_parts]
    for turn, slots in enumerate(turns):
        before = beside(ml, slots, 0)
        top = before
        for score in scores:
            top = jnp.maximum(top, jnp.max(score, axis=0, keepdims=True))
        keep = jnp.exp2((before - top) * scale)
        total = beside(ml, slots, 1) * keep
        mix = beside(ot, slots) * keep
        weights, following = [], []
        for k, score in enumerate(scores):
            if turn + 1 < len(turns):
                following.append(scores_of(key_parts[k], turns[turn + 1]))
            weight = jnp.exp2((score - top) * scale)
            total = total + jnp.sum(weight, axis=0, keepdims=True)
            weights.append(weight.astype(BF16))
        weights = weights[0] if len(weights) == 1 else jnp.concatenate(weights, axis=0)
        mix = mix + nn(vt[:, 0 : len(pieces) * half], weights)
        scores = following
        put([slots], [top], [total], [None])
        for some, mix in [(slots, mix)]:
            every = nn(vut[...], mix.astype(BF16))
            for k, s in enumerate(some):
                mine = every[:, k * group : (k + 1) * group]
                values = mine[0:LANES]
                for h in range(1, hs):
                    values = jnp.where(of_head == h, mine[h * LANES : (h + 1) * LANES], values)
                if s:
                    u_snd[s] = values.astype(BF16)
                else:
                    own_values = values
        for s in slots:
            if s:
                for copy in back(s):
                    copy.start()

    top = ml[0, 0:1, :]
    for s in range(1, nz):
        for copy in back(s):
            copy.wait_recv()
        top = jnp.maximum(top, ml_rcv[s, 0:1, :])
    keep = jnp.exp2((ml[0, 0:1, :] - top) * scale)
    numerator = own_values * keep
    denominator = ml[0, 1:2, :] * keep
    for s in range(1, nz):
        keep = jnp.exp2((ml_rcv[s, 0:1, :] - top) * scale)
        numerator = numerator + u_rcv[s].astype(F32) * keep
        denominator = denominator + ml_rcv[s, 1:2, :] * keep
    values = (numerator / denominator).T.astype(BF16)
    o_snd[...] = values.reshape(hs, ny, tr, LANES)
    own_heads = pl.ds(y * hs, hs)
    back_y = [
        remote(o_snd.at[:, up(y, d, ny)], o_rcv.at[own_heads], h_ssem.at[d], h_rsem.at[d], y_peer[d])
        for d in range(1, ny)
    ]
    for copy in back_y:
        copy.start()
    o_rcv[own_heads] = o_snd[:, y]
    for copy in back_y:
        copy.wait_recv()
    for h in range(heads):
        of[:, h, :] = o_rcv[h].astype(F32)
    hv[...] = of[...].astype(BF16)
    hv_copy = pltpu.make_async_copy(hv, hv_o, o_sem.at[2 * CORES])
    hv_copy.start()

    a_copy.wait_send()
    for copy in q1 + n1 + list(b.values()) + back_y:
        copy.wait_send()
    for k in range(1, nz):
        for d in range(ny):
            z_copy(d, k).wait_send()
    for s in range(1, nz):
        for copy in back(s):
            copy.wait_send()
    for e, u in [(e, u) for e in range(nx) for u in range(CUTS)]:
        if e:
            x_copy(0, e, u).wait_send()
            for d in y_far:
                x_copy(y_place[d], e, u).wait_send()
        to_sibling(e, u).wait_send()
        for d in y_near + (y_far if e == 0 else []):
            y_copy(d, e, u).wait_send()
    for copy in forwards:
        copy.wait_send()
    for copy in outs:
        copy.wait()
    hv_copy.wait()


def place_outputs(a, b, c, a_out, b_out, c_out, sem):
    copies = [pltpu.make_async_copy(i, o, sem.at[k]) for k, (i, o) in enumerate(((a, a_out), (b, b_out), (c, c_out)))]
    for copy in copies:
        copy.start()
    for copy in copies:
        copy.wait()


def local(
    prompt_hidden,
    latent_down,
    rope_down,
    latent_gain,
    request_lengths,
    row_request,
    query_nope,
    query_rope,
    new_latent,
    new_rope,
    key_up,
    value_up,
):
    ny = Y_SIZE
    nz = lax.axis_size("ctx") // ny
    nx = lax.axis_size("head") // CORES
    tok, depth = prompt_hidden.shape
    half = tok // CORES
    sl = half // nx
    steps, rows, heads, nope = query_nope.shape
    rope = query_rope.shape[-1]
    lat = key_up.shape[-1]
    tr = steps * rows
    hs = heads // ny
    group = hs * ny * tr
    wide = lat + LANES
    scale = math.log2(math.e) / math.sqrt(nope + rope)
    cfg = (nz, ny, nx, half, sl, lat, heads, hs, tr, rows, steps, group, rope, scale)
    spare = np.zeros((1, LANES), np.float32)
    frequency = 10000.0 ** (-2.0 * np.arange(rope // 2, dtype=np.float32) / rope)
    spare[0, :rope] = np.tile(frequency.astype(np.float32), 2)
    dma = pltpu.SemaphoreType.DMA
    vmem = pltpu.VMEM
    scratch = [
        vmem((2, half, depth), BF16),
        vmem((depth, lat), BF16),
        vmem((LANES, depth), BF16),
        vmem((1, lat), F32),
        vmem((tr, heads, nope), BF16),
        vmem((tr, heads, rope), BF16),
        vmem((steps, rows, lat), BF16),
        vmem((steps, rows, rope), BF16),
        vmem((hs, nope, lat), BF16),
        vmem((hs, lat, LANES), BF16),
        vmem((1, LANES), F32),
        dma((12,)),
        vmem((half, wide), BF16),
        vmem((half, wide), BF16),
        vmem((half, wide), F32),
        vmem((nx, sl, wide), BF16),
        vmem((nx, sl, wide), BF16),
        dma((2,)),
        dma((nx, CUTS)),
        dma((nx, CUTS)),
        vmem((CORES, ny, half, wide), BF16),
        vmem((lat, max(1, ny - 1) * tok), BF16),
        vmem((hs * LANES, lat), BF16),
        vmem((CORES, rope, half), BF16),
        dma((ny, nx, CUTS)),
        dma((ny, nx, CUTS)),
        dma((nx, CUTS)),
        dma((nx, CUTS)),
        dma((ny,)),
        dma((ny,)),
        dma((ny, nx, CUTS)),
        dma((ny, nx, CUTS)),
        dma((2 * CORES + 1,)),
        vmem((2, tr, heads, LANES), F32),
        vmem((ny, hs + hs // 2, tr, LANES), BF16),
        vmem((nz, ny, hs + hs // 2, tr, LANES), BF16),
        vmem((nz, group, wide), BF16),
        vmem((ny, tr, wide), BF16),
        dma((ny,)),
        dma((ny,)),
        dma((ny,)),
        dma((ny,)),
        dma((ny, nz)),
        dma((ny, nz)),
        vmem((nz, lat, group), F32),
        vmem((nz, 8, group), F32),
        vmem((nz, LANES, group), BF16),
        vmem((nz, LANES, group), BF16),
        vmem((nz, 8, group), F32),
        dma((nz,)),
        dma((nz,)),
        dma((nz,)),
        dma((nz,)),
        vmem((hs, ny, tr, LANES), BF16),
        vmem((heads, tr, LANES), BF16),
        vmem((tr, heads, LANES), F32),
        vmem((tr, heads, LANES), BF16),
        dma((ny,)),
        dma((ny,)),
    ]
    anywhere = pl.BlockSpec(memory_space=pl.ANY)
    scalars = pl.BlockSpec(memory_space=pltpu.SMEM)
    latent_cache, rope_cache, head_values = pl.pallas_call(
        functools.partial(kernel, cfg),
        out_shape=(
            jax.ShapeDtypeStruct((tok, lat), BF16),
            jax.ShapeDtypeStruct((rope, tok), BF16),
            jax.ShapeDtypeStruct((tr, heads, LANES), BF16),
        ),
        in_specs=[anywhere] * 4 + [scalars] * 2 + [anywhere] * 7,
        out_specs=(anywhere,) * 3,
        scratch_shapes=scratch,
        compiler_params=pltpu.CompilerParams(
            collective_id=0, has_side_effects=True, vmem_limit_bytes=60 * 1024 * 1024
        ),
    )(
        prompt_hidden,
        latent_down,
        rope_down,
        latent_gain.reshape(1, lat),
        request_lengths,
        row_request,
        query_nope.reshape(tr, heads, nope),
        query_rope.reshape(tr, heads, rope),
        new_latent,
        new_rope,
        key_up,
        value_up,
        jnp.asarray(spare),
    )
    latent_cache, rope_cache, head_values = pl.pallas_call(
        place_outputs,
        out_shape=tuple(jax.ShapeDtypeStruct(a.shape, a.dtype) for a in (latent_cache, rope_cache, head_values)),
        in_specs=[pl.BlockSpec(memory_space=pltpu.VMEM)] * 3,
        out_specs=(anywhere,) * 3,
        scratch_shapes=[dma((3,))],
    )(latent_cache, rope_cache, head_values)
    return (latent_cache, rope_cache, head_values.reshape(steps, rows, heads, LANES))


def solution(mesh):
    placed = (
        P("ctx", "head"),
        P("head", None),
        P(None, "head"),
        P(),
        P(),
        P(),
        P(None, "ctx", "head", None),
        P(None, "ctx", "head", None),
        P(None, "ctx", None),
        P(None, "ctx", None),
        P("head", None, None),
        P("head", None, None),
    )
    return jax.shard_map(
        local,
        mesh=mesh,
        in_specs=placed,
        out_specs=(P("ctx", None), P(None, "ctx"), P(None, "ctx", "head", None)),
        check_vma=False,
    )
```

```python
import functools
import math

import jax
import jax.numpy as jnp
import numpy as np
from jax import lax
from jax.experimental import pallas as pl
from jax.experimental.pallas import tpu as pltpu
from jax.sharding import PartitionSpec as P

MESH = pl.DeviceIdType.MESH
EPSILON = 1e-6
MASKED = -1e30
Y_SIZE = 4
CORES = 2
LANES = 128
CUTS = 2
LAST_AT_ONCE = 2
PART = 2
JOIN = 2
AT_ONCE = 4
F32 = jnp.float32
BF16 = jnp.bfloat16


def nt(a, b):
    return lax.dot_general(a, b, (((1,), (1,)), ((), ())), preferred_element_type=F32)


def nn(a, b):
    return jnp.dot(a, b, preferred_element_type=F32)


def kernel(
    cfg,
    hid_h, ld_h, rd_h, gain_h, lens, rowreq, qn_h, qr_h, nl_h, nr_h, ku_h, vu_h, freq_h,
    lat_o, rope_o, hv_o,
    hid, ld, rd, gain, qn, qr, nl, nr, ku, vu, freq, loc,
    a_snd, a_rcv, part, b_snd, b_rcv, a_sem, b_ssem, b_rsem,
    kv, vt, vt_own, vut, rope_t, x_ssem, x_rsem, s0_ssem, s0_rsem, s_ssem, s_rsem, y_ssem, y_rsem, o_sem,
    qf, q_snd, qg, qa, nkv, q1_ssem, q1_rsem, n1_ssem, n1_rsem, q2_ssem, q2_rsem,
    ot, ml, u_snd, u_rcv, ml_rcv, u_ssem, u_rsem, m_ssem, m_rsem,
    o_snd, o_rcv, of, hv, h_ssem, h_rsem,
):
    nz, ny, nx, half, sl, lat, heads, hs, tr, rows, steps, group, rope, scale = cfg
    wide = lat + LANES
    ctx = lax.axis_index("ctx")
    head = lax.axis_index("head")
    z, y = ctx // ny, ctx % ny
    x, c = head // CORES, head % CORES

    def dev(zz, yy, xx, cc):
        return (zz * ny + yy, xx * CORES + cc)

    def up(value, by, size):
        return (value + by) % size

    def remote(src, dst, ssem, rsem, device):
        return pltpu.make_async_remote_copy(
            src_ref=src, dst_ref=dst, send_sem=ssem, recv_sem=rsem, device_id=device, device_id_type=MESH
        )

    sibling = dev(z, y, x, 1 - c)
    x_peer = [None] + [dev(z, y, up(x, d, nx), c) for d in range(1, nx)]
    y_peer = [None] + [dev(z, up(y, d, ny), x, c) for d in range(1, ny)]

    y_order = [0, 1] + ([ny - 1] + list(range(2, ny - 1)) if ny > 2 else [])
    y_place = {d: i for i, d in enumerate(y_order)}
    y_near = y_order[1:3]
    y_far = y_order[3:]

    loads = [
        (qn_h, qn),
        (qr_h, qr),
        (hid_h.at[pl.ds(pl.multiple_of((1 - c) * half, half), half)], hid.at[0]),
        (ld_h, ld),
        (rd_h, rd.at[pl.ds(0, rope)]),
        (hid_h.at[pl.ds(pl.multiple_of(c * half, half), half)], hid.at[1]),
        (nl_h, nl),
        (nr_h, nr),
        (gain_h, gain),
        (freq_h, freq),
        (ku_h.at[pl.ds(y * hs, hs)], ku),
        (vu_h.at[pl.ds(y * hs, hs)], vu),
    ]
    loads = [pltpu.make_async_copy(src, dst, loc.at[i]) for i, (src, dst) in enumerate(loads)]
    for load in loads:
        load.start()

    barrier = pltpu.get_barrier_semaphore()
    peers = [sibling] + x_peer[1:] + y_peer[1:] + [dev(up(z, d, nz), y, x, c) for d in range(1, nz)]
    for peer in peers:
        pl.semaphore_signal(barrier, inc=1, device_id=peer, device_id_type=MESH)

    loads[0].wait()
    loads[1].wait()
    qf[0] = qn[...].astype(F32)
    qf[1, :, :, 0:rope] = qr[...].astype(F32)
    lane = lax.broadcasted_iota(jnp.int32, (tr, LANES), 1)
    for h in range(heads):
        q_snd[h // hs, h % hs] = qf[0, :, h, :].astype(BF16)
    for h in range(0, heads, 2):
        pair = jnp.where(lane < rope, qf[1, :, h, :], pltpu.roll(qf[1, :, h + 1, :], rope, 1))
        q_snd[h // hs, hs + (h % hs) // 2] = pair.astype(BF16)
    qg[0, y] = q_snd[y]
    loads[6].wait()
    loads[7].wait()
    nkv[y, :, 0:lat] = nl[...].reshape(tr, lat)
    nkv[y, :, lat:] = jnp.zeros((tr, LANES), BF16)
    nkv[y, :, lat : lat + rope] = nr[...].reshape(tr, rope)

    rd[pl.ds(rope, LANES - rope)] = jnp.zeros((LANES - rope, rd.shape[1]), BF16)
    for i in (2, 3, 4):
        loads[i].wait()
    a_snd[:, 0:lat] = nn(hid[0], ld[...]).astype(BF16)
    a_snd[:, lat:] = nt(hid[0], rd[...]).astype(BF16)

    pl.semaphore_wait(barrier, len(peers))
    a_copy = remote(a_snd, a_rcv, a_sem.at[0], a_sem.at[1], sibling)
    a_copy.start()
    q1, n1 = [], []
    for d in range(1, ny):
        to = up(y, d, ny)
        q1.append(
            remote(q_snd.at[to], qg.at[0, y], q1_ssem.at[d], q1_rsem.at[d], y_peer[d])
        )
        n1.append(remote(nkv.at[y], nkv.at[y], n1_ssem.at[d], n1_rsem.at[d], y_peer[d]))
    z_order = [(i + 1) // 2 if i % 2 else (nz - i // 2) % nz for i in range(nz)]

    def z_copy(d, k):
        source = up(y, ny - d, ny)
        return remote(
            qg.at[0, source],
            qg.at[k, source],
            q2_ssem.at[d, k],
            q2_rsem.at[d, k],
            dev(up(z, k, nz), y, x, c),
        )

    for copy in q1:
        copy.start()
    for k in z_order[1:]:
        z_copy(0, k).start()

    loads[5].wait()
    part[:, 0:lat] = nn(hid[1], ld[...])
    part[:, lat:] = nt(hid[1], rd[...])

    a_copy.wait_recv()
    part[...] += a_rcv[...].astype(F32)
    b_snd[...] = part[...].astype(BF16).reshape(nx, sl, wide)
    cut = sl // CUTS
    x_order = ([1, nx - 1] + list(range(2, nx - 1))) if nx > 2 else list(range(1, nx))
    b = {}
    for u in range(CUTS):
        for d in x_order:
            rows_u = pl.ds(u * cut, cut)
            b[d, u] = remote(
                b_snd.at[up(x, d, nx), rows_u], b_rcv.at[d, rows_u], b_ssem.at[d, u], b_rsem.at[d, u], x_peer[d]
            )
            b[d, u].start()
    for copy in n1:
        copy.start()
    for d in range(1, ny):
        q1[d - 1].wait_recv()
        for k in z_order[1:]:
            z_copy(d, k).start()

    loads[11].wait()
    for h in range(hs):
        vut[pl.ds(h * LANES, LANES)] = vu[h].T
    loads[8].wait()
    loads[9].wait()
    position = (ctx * (half * CORES) + c * half + x * sl) + lax.broadcasted_iota(jnp.int32, (sl, LANES), 0)
    owner = jnp.zeros((sl, LANES), jnp.int32)
    start = jnp.zeros((sl, LANES), jnp.int32)
    end = jnp.int32(0)
    for r in range(lens.shape[0] - 1):
        end = end + lens[r]
        owner = owner + jnp.where(position >= end, 1, 0)
        start = jnp.where(position >= end, end, start)
    angle = freq[...] * (position - start).astype(F32)
    cosine, sine = jnp.cos(angle), jnp.sin(angle)
    lane = lax.broadcasted_iota(jnp.int32, (sl, LANES), 1)
    penalty = jnp.where((lane >= rope) & (lane < rope + lens.shape[0]) & (lane - rope != owner), MASKED, 0.0)

    def rows_of(e, u):
        return pl.ds(pl.multiple_of(up(x, nx - e, nx) * sl + u * cut, cut), cut)

    def x_copy(p, e, u):
        place = kv.at[0, p, rows_of(0, u)]
        return remote(place, place, x_ssem.at[p, e, u], x_rsem.at[p, e, u], x_peer[e])

    def to_sibling(e, u):
        there = rows_of(e, u)
        return remote(kv.at[0, 0, there], kv.at[1, 0, there], s0_ssem.at[e, u], s0_rsem.at[e, u], sibling)

    def y_copy(d, e, u):
        there = rows_of(e, u)
        return remote(
            kv.at[0, 0, there], kv.at[0, y_place[d], there], y_ssem.at[d, e, u], y_rsem.at[d, e, u], y_peer[d]
        )

    for u in range(CUTS):
        some = slice(u * cut, (u + 1) * cut)
        total = part[rows_of(0, u), :]
        for d in x_order:
            b[d, u].wait_recv()
            total = total + b_rcv[d, some].astype(F32)
        latent = total[:, 0:lat]
        mean_square = jnp.mean(latent * latent, axis=-1, keepdims=True)
        kv[0, 0, rows_of(0, u), 0:lat] = (latent * lax.rsqrt(mean_square + EPSILON) * gain[...]).astype(BF16)
        raw = total[:, lat:]
        low = lane[some] < rope // 2
        turned = jnp.where(low, -pltpu.roll(raw, LANES - rope // 2, 1), pltpu.roll(raw, rope // 2, 1))
        rotated = jnp.where(lane[some] < rope, raw * cosine[some] + turned * sine[some], penalty[some])
        kv[0, 0, rows_of(0, u), lat:] = rotated.astype(BF16)
        for e in x_order:
            x_copy(0, e, u).start()
        to_sibling(0, u).start()
        for d in y_order[1:]:
            y_copy(d, 0, u).start()
    for u in range(CUTS):
        for e in x_order:
            x_copy(0, e, u).wait_recv()
            for d in y_near:
                y_copy(d, e, u).start()
            to_sibling(e, u).start()
        for d in y_far:
            y_copy(d, 0, u).wait_recv()
            for e in x_order:
                x_copy(y_place[d], e, u).start()

    ml[...] = jnp.zeros(ml.shape, F32)
    for copy in n1:
        copy.wait_recv()
    loads[10].wait()
    for u in range(CUTS):
        for e in range(nx):
            to_sibling(e, u).wait_recv()

    def chunk_keys(pieces):
        return jnp.concatenate([kv[i, j] for i, j in pieces], axis=0)

    def transpose_values(pieces, first=0):
        for k, (i, j) in enumerate(pieces):
            vt[:, (first + k) * half : (first + k + 1) * half] = kv[i, j, :, 0:lat].T

    per_head = ny * tr
    lane = lax.broadcasted_iota(jnp.int32, (per_head, LANES), 1)
    line = lax.broadcasted_iota(jnp.int32, (per_head, LANES), 0)

    def absorb(s):
        first_row = up(z, nz - s, nz) * (ny * rows)
        request = jnp.zeros((per_head, LANES), jnp.int32)
        for i in range(ny * rows):
            here = (line // tr == i // rows) & (line % rows == i % rows)
            request = jnp.where(here, rowreq[first_row + i], request)
        one_hot = jnp.where(lane - rope == request, 1.0, 0.0)
        for h in range(hs):
            here = pl.ds(h * per_head, per_head)
            qa[s, here, 0:lat] = nn(qg[s, :, h].reshape(per_head, LANES), ku[h]).astype(BF16)
            pair = qg[s, :, hs + h // 2].reshape(per_head, LANES).astype(F32)
            if h % 2:
                pair = pltpu.roll(pair, rope, 1)
            qa[s, here, lat:] = jnp.where(lane < rope, pair, one_hot).astype(BF16)

    def joined(slots):
        return [slots[i : i + JOIN] for i in range(0, len(slots), JOIN)]

    def beside(ref, slots, row=None):
        parts = [ref[s] if row is None else ref[s, row : row + 1, :] for s in slots]
        return parts[0] if len(parts) == 1 else jnp.concatenate(parts, axis=1)

    def scores_of(keys, slots):
        parts = [qa[s] for s in slots]
        return nt(keys, parts[0] if len(parts) == 1 else jnp.concatenate(parts, axis=0))

    def first_keys(keys, values, bunch):
        scores = [scores_of(keys, slots) for slots in bunch]
        tops = [jnp.max(score, axis=0, keepdims=True) for score in scores]
        weights = [jnp.exp2((score - top) * scale) for score, top in zip(scores, tops)]
        sums = [jnp.sum(weight, axis=0, keepdims=True) for weight in weights]
        mixed = [nn(values, weight.astype(BF16)) for weight in weights]
        return tops, sums, mixed

    def next_keys(scores, values, bunch):
        before = [beside(ml, slots, 0) for slots in bunch]
        sums = [beside(ml, slots, 1) for slots in bunch]
        tops = [jnp.maximum(old, jnp.max(score, axis=0, keepdims=True)) for old, score in zip(before, scores)]
        weights = [jnp.exp2((score - top) * scale) for score, top in zip(scores, tops)]
        keeps = [jnp.exp2((old - top) * scale) for old, top in zip(before, tops)]
        sums = [
            old * keep + jnp.sum(weight, axis=0, keepdims=True) for old, keep, weight in zip(sums, keeps, weights)
        ]
        mixed = [
            beside(ot, slots) * keep + nn(values, weight.astype(BF16))
            for slots, keep, weight in zip(bunch, keeps, weights)
        ]
        return tops, sums, mixed

    def put(bunch, tops, sums, mixed):
        for slots, top, total, mix in zip(bunch, tops, sums, mixed):
            for k, s in enumerate(slots):
                here = slice(k * group, (k + 1) * group)
                ml[s, 0:1, :] = top[:, here]
                ml[s, 1:2, :] = total[:, here]
                if mix is not None:
                    ot[s] = mix[:, here]

    at_once = min(AT_ONCE, nz)
    bunches = [z_order[i : i + at_once] for i in range(0, nz, at_once)]
    own_pieces = [(0, 0), (1, 0)]
    for i, j in own_pieces:
        vt_own[:, i * half : (i + 1) * half] = kv[i, j, :, 0:lat].T

    def visit_own(slots):
        for s in slots:
            if s:
                for d in range(ny):
                    z_copy(d, s).wait_recv()
            absorb(s)
        bunch = joined(slots)
        put(bunch, *first_keys(chunk_keys(own_pieces), vt_own[...], bunch))

    visit_own(bunches[0])

    sides = [c, 1 - c]
    outs = []
    for i in range(CORES):
        rope_t[i] = kv[i, 0, :, lat:].astype(F32).T[0:rope].astype(BF16)
        place = pl.ds(pl.multiple_of(sides[i] * half, half), half)
        outs.append(pltpu.make_async_copy(kv.at[i, 0, :, pl.ds(0, lat)], lat_o.at[place], o_sem.at[2 * i]))
        outs.append(pltpu.make_async_copy(rope_t.at[i], rope_o.at[:, place], o_sem.at[2 * i + 1]))
    for copy in outs:
        copy.start()

    fresh = ny * tr
    new_keys = nkv[...].reshape(fresh, wide)
    key_of = lax.broadcasted_iota(jnp.int32, (fresh, group), 0)
    query_of = lax.broadcasted_iota(jnp.int32, (fresh, group), 1) % fresh
    allowed = (
        (key_of // tr == query_of // tr)
        & (key_of % rows == query_of % rows)
        & ((key_of % tr) // rows <= (query_of % tr) // rows)
    )
    scores = jnp.where(allowed, nt(new_keys, qa[0]), MASKED)
    put([[0]], *next_keys([scores], new_keys[:, 0:lat].astype(F32).T.astype(BF16), [[0]]))

    pieces = [(i, p) for i in range(CORES) for p in range(1, ny)]
    forwards = []
    for p in range(1, ny):
        d = y_order[p]
        for u in range(CUTS):
            for e in range(1, nx):
                if d in y_near:
                    y_copy(d, e, u).wait_recv()
                else:
                    x_copy(p, e, u).wait_recv()
            if d in y_near:
                y_copy(d, 0, u).wait_recv()
        forwards.append(remote(kv.at[0, p], kv.at[1, p], s_ssem.at[p], s_rsem.at[p], sibling))
        forwards[-1].start()
    for slots in bunches[1:]:
        visit_own(slots)
    transpose_values(pieces[: ny - 1])
    for copy in forwards:
        copy.wait_recv()
    transpose_values(pieces[ny - 1 :], ny - 1)

    def back(s):
        to = dev(up(z, nz - s, nz), y, x, c)
        return (
            remote(u_snd.at[s], u_rcv.at[s], u_ssem.at[s], u_rsem.at[s], to),
            remote(ml.at[s, pl.ds(0, 2)], ml_rcv.at[s, pl.ds(0, 2)], m_ssem.at[s], m_rsem.at[s], to),
        )

    of_head = lax.broadcasted_iota(jnp.int32, (LANES, group), 1) // (group // hs)
    own_values = None
    last_order = z_order[::-1]
    if nz == 8:
        last_order = [3, 5, 4, 6, 2, 7, 1, 0]
    turns = [last_order[i : i + LAST_AT_ONCE] for i in range(0, nz, LAST_AT_ONCE)]
    key_parts = [chunk_keys(pieces[k : k + PART]) for k in range(0, len(pieces), PART)]
    scores = [scores_of(keys, turns[0]) for keys in key_parts]
    for turn, slots in enumerate(turns):
        before = beside(ml, slots, 0)
        top = before
        for score in scores:
            top = jnp.maximum(top, jnp.max(score, axis=0, keepdims=True))
        keep = jnp.exp2((before - top) * scale)
        total = beside(ml, slots, 1) * keep
        mix = beside(ot, slots) * keep
        weights, following = [], []
        for k, score in enumerate(scores):
            if turn + 1 < len(turns):
                following.append(scores_of(key_parts[k], turns[turn + 1]))
            weight = jnp.exp2((score - top) * scale)
            total = total + jnp.sum(weight, axis=0, keepdims=True)
            weights.append(weight.astype(BF16))
        weights = weights[0] if len(weights) == 1 else jnp.concatenate(weights, axis=0)
        mix = mix + nn(vt[:, 0 : len(pieces) * half], weights)
        scores = following
        put([slots], [top], [total], [None])
        for some, mix in [(slots, mix)]:
            every = nn(vut[...], mix.astype(BF16))
            for k, s in enumerate(some):
                mine = every[:, k * group : (k + 1) * group]
                values = mine[0:LANES]
                for h in range(1, hs):
                    values = jnp.where(of_head == h, mine[h * LANES : (h + 1) * LANES], values)
                if s:
                    u_snd[s] = values.astype(BF16)
                else:
                    own_values = values
        for s in slots:
            if s:
                for copy in back(s):
                    copy.start()

    top = ml[0, 0:1, :]
    for s in range(1, nz):
        for copy in back(s):
            copy.wait_recv()
        top = jnp.maximum(top, ml_rcv[s, 0:1, :])
    keep = jnp.exp2((ml[0, 0:1, :] - top) * scale)
    numerator = own_values * keep
    denominator = ml[0, 1:2, :] * keep
    for s in range(1, nz):
        keep = jnp.exp2((ml_rcv[s, 0:1, :] - top) * scale)
        numerator = numerator + u_rcv[s].astype(F32) * keep
        denominator = denominator + ml_rcv[s, 1:2, :] * keep
    values = (numerator / denominator).T.astype(BF16)
    values = values.reshape(hs, ny, tr, LANES)
    for i in range(ny):
        o_snd[i] = values[:, i]
    own_heads = pl.ds(y * hs, hs)
    back_y = [
        remote(o_snd.at[up(y, d, ny)], o_rcv.at[own_heads], h_ssem.at[d], h_rsem.at[d], y_peer[d])
        for d in range(1, ny)
    ]
    for copy in back_y:
        copy.start()
    o_rcv[own_heads] = o_snd[y]
    for copy in back_y:
        copy.wait_recv()
    for h in range(heads):
        of[:, h, :] = o_rcv[h].astype(F32)
    hv[...] = of[...].astype(BF16)
    hv_copy = pltpu.make_async_copy(hv, hv_o, o_sem.at[2 * CORES])
    hv_copy.start()

    a_copy.wait_send()
    for copy in q1 + n1 + list(b.values()) + back_y:
        copy.wait_send()
    for k in range(1, nz):
        for d in range(ny):
            z_copy(d, k).wait_send()
    for s in range(1, nz):
        for copy in back(s):
            copy.wait_send()
    for e, u in [(e, u) for e in range(nx) for u in range(CUTS)]:
        if e:
            x_copy(0, e, u).wait_send()
            for d in y_far:
                x_copy(y_place[d], e, u).wait_send()
        to_sibling(e, u).wait_send()
        for d in y_near + (y_far if e == 0 else []):
            y_copy(d, e, u).wait_send()
    for copy in forwards:
        copy.wait_send()
    for copy in outs:
        copy.wait()
    hv_copy.wait()


def place_outputs(a, b, c, a_out, b_out, c_out, sem):
    copies = [pltpu.make_async_copy(i, o, sem.at[k]) for k, (i, o) in enumerate(((a, a_out), (b, b_out), (c, c_out)))]
    for copy in copies:
        copy.start()
    for copy in copies:
        copy.wait()


def local(
    prompt_hidden,
    latent_down,
    rope_down,
    latent_gain,
    request_lengths,
    row_request,
    query_nope,
    query_rope,
    new_latent,
    new_rope,
    key_up,
    value_up,
):
    ny = Y_SIZE
    nz = lax.axis_size("ctx") // ny
    nx = lax.axis_size("head") // CORES
    tok, depth = prompt_hidden.shape
    half = tok // CORES
    sl = half // nx
    steps, rows, heads, nope = query_nope.shape
    rope = query_rope.shape[-1]
    lat = key_up.shape[-1]
    tr = steps * rows
    hs = heads // ny
    group = hs * ny * tr
    wide = lat + LANES
    scale = math.log2(math.e) / math.sqrt(nope + rope)
    cfg = (nz, ny, nx, half, sl, lat, heads, hs, tr, rows, steps, group, rope, scale)
    spare = np.zeros((1, LANES), np.float32)
    frequency = 10000.0 ** (-2.0 * np.arange(rope // 2, dtype=np.float32) / rope)
    spare[0, :rope] = np.tile(frequency.astype(np.float32), 2)
    dma = pltpu.SemaphoreType.DMA
    vmem = pltpu.VMEM
    scratch = [
        vmem((2, half, depth), BF16),
        vmem((depth, lat), BF16),
        vmem((LANES, depth), BF16),
        vmem((1, lat), F32),
        vmem((tr, heads, nope), BF16),
        vmem((tr, heads, rope), BF16),
        vmem((steps, rows, lat), BF16),
        vmem((steps, rows, rope), BF16),
        vmem((hs, nope, lat), BF16),
        vmem((hs, lat, LANES), BF16),
        vmem((1, LANES), F32),
        dma((12,)),
        vmem((half, wide), BF16),
        vmem((half, wide), BF16),
        vmem((half, wide), F32),
        vmem((nx, sl, wide), BF16),
        vmem((nx, sl, wide), BF16),
        dma((2,)),
        dma((nx, CUTS)),
        dma((nx, CUTS)),
        vmem((CORES, ny, half, wide), BF16),
        vmem((lat, max(1, ny - 1) * tok), BF16),
        vmem((lat, tok), BF16),
        vmem((hs * LANES, lat), BF16),
        vmem((CORES, rope, half), BF16),
        dma((ny, nx, CUTS)),
        dma((ny, nx, CUTS)),
        dma((nx, CUTS)),
        dma((nx, CUTS)),
        dma((ny,)),
        dma((ny,)),
        dma((ny, nx, CUTS)),
        dma((ny, nx, CUTS)),
        dma((2 * CORES + 1,)),
        vmem((2, tr, heads, LANES), F32),
        vmem((ny, hs + hs // 2, tr, LANES), BF16),
        vmem((nz, ny, hs + hs // 2, tr, LANES), BF16),
        vmem((nz, group, wide), BF16),
        vmem((ny, tr, wide), BF16),
        dma((ny,)),
        dma((ny,)),
        dma((ny,)),
        dma((ny,)),
        dma((ny, nz)),
        dma((ny, nz)),
        vmem((nz, lat, group), F32),
        vmem((nz, 8, group), F32),
        vmem((nz, LANES, group), BF16),
        vmem((nz, LANES, group), BF16),
        vmem((nz, 8, group), F32),
        dma((nz,)),
        dma((nz,)),
        dma((nz,)),
        dma((nz,)),
        vmem((ny, hs, tr, LANES), BF16),
        vmem((heads, tr, LANES), BF16),
        vmem((tr, heads, LANES), F32),
        vmem((tr, heads, LANES), BF16),
        dma((ny,)),
        dma((ny,)),
    ]
    anywhere = pl.BlockSpec(memory_space=pl.ANY)
    scalars = pl.BlockSpec(memory_space=pltpu.SMEM)
    latent_cache, rope_cache, head_values = pl.pallas_call(
        functools.partial(kernel, cfg),
        out_shape=(
            jax.ShapeDtypeStruct((tok, lat), BF16),
            jax.ShapeDtypeStruct((rope, tok), BF16),
            jax.ShapeDtypeStruct((tr, heads, LANES), BF16),
        ),
        in_specs=[anywhere] * 4 + [scalars] * 2 + [anywhere] * 7,
        out_specs=(anywhere,) * 3,
        scratch_shapes=scratch,
        compiler_params=pltpu.CompilerParams(
            collective_id=0, has_side_effects=True, vmem_limit_bytes=60 * 1024 * 1024
        ),
    )(
        prompt_hidden,
        latent_down,
        rope_down,
        latent_gain.reshape(1, lat),
        request_lengths,
        row_request,
        query_nope.reshape(tr, heads, nope),
        query_rope.reshape(tr, heads, rope),
        new_latent,
        new_rope,
        key_up,
        value_up,
        jnp.asarray(spare),
    )
    latent_cache, rope_cache, head_values = pl.pallas_call(
        place_outputs,
        out_shape=tuple(jax.ShapeDtypeStruct(a.shape, a.dtype) for a in (latent_cache, rope_cache, head_values)),
        in_specs=[pl.BlockSpec(memory_space=pltpu.VMEM)] * 3,
        out_specs=(anywhere,) * 3,
        scratch_shapes=[dma((3,))],
    )(latent_cache, rope_cache, head_values)
    return (latent_cache, rope_cache, head_values.reshape(steps, rows, heads, LANES))


def solution(mesh):
    placed = (
        P("ctx", "head"),
        P("head", None),
        P(None, "head"),
        P(),
        P(),
        P(),
        P(None, "ctx", "head", None),
        P(None, "ctx", "head", None),
        P(None, "ctx", None),
        P(None, "ctx", None),
        P("head", None, None),
        P("head", None, None),
    )
    return jax.shard_map(
        local,
        mesh=mesh,
        in_specs=placed,
        out_specs=(P("ctx", None), P(None, "ctx"), P(None, "ctx", "head", None)),
        check_vma=False,
    )
```
